32 devices in a mesh: grp: 2 (over y), bin: 4 (over z), off: 2 (over x), sub: 2 (over core).
Axes of the slice: x: 2, y: 2, z: 4, core: 2. Of those that a mesh axis runs over, the one named last changes fastest.
Arguments:
- traces: bfloat16 [4, 4096, 2048], P(('grp', 'off'), ('bin', 'sub')), parts along dimension 0, may hold values from -6 to 6
- mid_bin: int32 [4, 4096], P(('grp', 'off'), ('bin', 'sub')), parts along dimension 0, may hold values from 0 to 2047, as said below
- live_count: int32 [4, 8], P(('grp', 'off'), ('bin', 'sub')), parts along dimension 0, may hold values from 256 to 512, as said below
- fine_class: int32 [4, 4096], P(('grp', 'off'), ('bin', 'sub')), parts along dimension 0, may hold values from 0 to 1
- operator: bfloat16 [4, 2, 4, 8, 8, 128, 128], P(('grp', 'off'), None, 'bin', 'sub'), parts along dimension 0, may hold values from -0.1875 to 0.1875
- block_index: int32 [4, 2, 4, 8, 8], P(('grp', 'off'), None, 'bin', 'sub'), parts along dimension 0, may hold values from 0 to 15
Outputs:
- image: float32 [4096, 1024], P(('grp', 'bin', 'off'), 'sub'), parts along dimension 0
The draws below stay inside these ranges and needn't reach their ends.
There are 2 independent parts, one for each index of `grp`. The reference program is written for one: setup_inputs(seed, part) draws one part's arguments, and reference() takes and returns one part's arrays. A program takes and returns all parts, laid end to end along the dimension named above; each array names one. Nothing has to cross between parts.
Inputs may be any that keep to these rules, and one draw needn't show every extreme that they name: `mid_bin`: among the live rows of one shot-order device at most 192 lie in the bins of one owner (bins o * 512 to o * 512 + 511), and on every device some owner has exactly 192. `live_count`: some device holds 512 live rows in every draw.
All inputs are finite; a program needn't handle non-finite values.
Results may differ from the reference program's by a relative error of at most 0.0023.
Values may be sent and summed in bfloat16 or wider, within the bound.
No kernel may reach another device: no remote copies, remote signals or barrier semaphores. Data moves between devices by JAX's collectives and lax.ppermute only.
A program may use at most 64 MiB of HBM per device.

```python
import jax
import jax.numpy as jnp
from jax import lax

TS = 2048
BLK = 128
SB = 16
DB = 8
K = 8
FINE = 2
COLS = 512
TR_DEV = 512
NOFF = 2
SRC = 8
ROWS = 4096
NCOL = 2048
DEPTH = 1024
CAP = 192
N_BIN = 4


def owner_block(key):
    first, second, third, fourth = jax.random.split(key, 4)
    heavy = jax.random.randint(first, (), 0, N_BIN)
    others = jax.random.permutation(second, (N_BIN - 1) * CAP)[:TR_DEV - CAP] // CAP
    others = others + (others >= heavy).astype(jnp.int32)
    half = TR_DEV // 2
    front = jnp.concatenate([jnp.full((CAP,), heavy, jnp.int32), others[:half - CAP].astype(jnp.int32)])
    front = front[jax.random.permutation(third, half)]
    owner = jnp.concatenate([front, others[half - CAP:].astype(jnp.int32)])
    column = jax.random.randint(fourth, (TR_DEV,), 0, COLS)
    return (owner * COLS + column).astype(jnp.int32)


def draw_mid_bin(key, part):
    key = jax.random.fold_in(key, 11)
    keys = jax.random.split(key, NOFF * SRC)
    return jax.vmap(owner_block)(keys).reshape(NOFF, SRC * TR_DEV)


def draw_live_count(key, part):
    key = jax.random.fold_in(key, 23)
    first, second = jax.random.split(key)
    counts = jax.random.randint(first, (NOFF * SRC,), TR_DEV // 2, TR_DEV + 1)
    filled = jax.random.randint(second, (), 0, NOFF * SRC)
    return counts.at[filled].set(TR_DEV).reshape(NOFF, SRC).astype(jnp.int32)


def plant(entries, rng, low, high):
    shape = entries.shape
    index_at = [jax.random.randint(jax.random.fold_in(rng, axis), (), 0, shape[axis]) for axis in range(len(shape))]
    entries = entries.at[tuple(index_at)].set(low)
    longest = shape.index(max(shape))
    index_at[longest] = (index_at[longest] + 1) % shape[longest]
    return entries.at[tuple(index_at)].set(high)


def block_levels(own_key, shape, shards, smallest, top_value):
    gain = 1.0
    for axis_at, shards_of in shards:
        draws = jax.random.uniform(jax.random.fold_in(jax.random.fold_in(own_key, 6), axis_at), (shards_of,), jnp.float32, smallest / len(shards), top_value / len(shards))
        gain = gain * jnp.repeat(jnp.exp(draws), shape[axis_at] // shards_of).reshape((-1,) + (1,) * (len(shape) - 1 - axis_at))
    return gain


def centred(own_key, shape, spread, limit, cuts=(), kind=jnp.bfloat16):
    drawn = spread * jax.random.normal(own_key, shape, jnp.float32)
    if cuts:
        drawn = drawn * block_levels(own_key, shape, cuts, -0.22, 0.18)
    return jnp.clip(drawn, -limit, limit).astype(kind)


def setup_inputs(seed: int = 0, part: int = 0) -> dict:
    key_of = jax.random.split(jax.random.key(seed), 7)
    part_splits = jax.random.split(jax.random.fold_in(key_of[6], part), 7)
    traces = centred(part_splits[0], (NOFF, ROWS, TS), 1.0, 6.0, ((0, 2), (1, 8)))
    mid_bin = draw_mid_bin(jax.random.fold_in(jax.random.fold_in(key_of[6], part), 71), part)
    live_count = draw_live_count(jax.random.fold_in(jax.random.fold_in(key_of[6], part), 71), part)
    fine_class = plant(jax.random.randint(part_splits[3], (NOFF, ROWS), 0, FINE), jax.random.fold_in(part_splits[3], 1), 0, FINE - 1).astype(jnp.int32)
    operator = centred(part_splits[4], (NOFF, FINE, N_BIN, DB, K, BLK, BLK), (K * BLK) ** -0.5, 0.1875, ((0, 2), (2, 4), (3, 2)))
    block_index = plant(jax.random.randint(part_splits[5], (NOFF, FINE, N_BIN, DB, K), 0, SB), jax.random.fold_in(part_splits[5], 1), 0, SB - 1).astype(jnp.int32)
    return dict(traces=traces, mid_bin=mid_bin, live_count=live_count, fine_class=fine_class, operator=operator, block_index=block_index)


def pick_blocks(columns, chosen):
    return jnp.take(columns, chosen.reshape(-1), axis=1)


def reference(traces, mid_bin, live_count, fine_class, operator, block_index):
    records = traces.shape[1]
    per_device = records // live_count.shape[1]
    position = jnp.arange(records, dtype=jnp.int32) % per_device
    alive = position[None, :] < jnp.repeat(live_count, per_device, axis=1)
    segment = jnp.where(alive, fine_class * NCOL + mid_bin, FINE * NCOL).astype(jnp.int32)

    def one_group(carry, members):
        data, labels, group_ops, group_chosen = members
        stacked = jax.ops.segment_sum(data.astype(jnp.float32), labels, num_segments=FINE * NCOL + 1)[: FINE * NCOL]
        stacked = stacked.astype(jnp.bfloat16).reshape(FINE, N_BIN, COLS, SB, BLK)

        def one_owner(owner_members):
            block_data, block_ops, block_chosen = owner_members
            picked = jax.vmap(pick_blocks)(block_data, block_chosen)
            picked = picked.reshape(FINE, COLS, DB, K, BLK)
            return jnp.einsum("fcdkq,fdkpq->cdp", picked.astype(jnp.float32), block_ops.astype(jnp.float32))

        partial_image = lax.map(one_owner, (jnp.moveaxis(stacked, 1, 0), jnp.moveaxis(group_ops, 1, 0), jnp.moveaxis(group_chosen, 1, 0)))
        return carry + partial_image, None

    start_image = jnp.zeros((N_BIN, COLS, DB, BLK), jnp.float32)
    total, _ = lax.scan(one_group, start_image, (traces, segment, operator, block_index))
    return total.reshape(NCOL, DEPTH)
```

```python
import functools

import jax
import jax.numpy as jnp
from jax import lax
from jax.experimental import pallas as pl
from jax.experimental.pallas import tpu as pltpu
from jax.sharding import PartitionSpec as P

FINE = 2
COLS = 512
LABEL_ROWS = 16
TILE = 256
BF = jnp.bfloat16
F32 = jnp.float32
MIB = 1 << 20


def params(mib):
    return pltpu.CompilerParams(vmem_limit_bytes=mib * MIB)


def vmem():
    return pl.BlockSpec(memory_space=pltpu.VMEM)


def smem():
    return pl.BlockSpec(memory_space=pltpu.SMEM)


def pack_kernel(plan, live_ref, mid_ref, fine_ref, traces_ref, *outs):
    owners, subs, cap, start, width, labelled = plan
    z = lax.axis_index("bin")
    s = lax.axis_index("sub")
    rows, samples = traces_ref.shape
    half = samples // subs
    live = lax.broadcasted_iota(jnp.int32, (1, rows), 1) < live_ref[0, 0]
    mid = mid_ref[...]
    owner = mid // COLS
    group = max(owners, 16)
    target = lax.broadcasted_iota(jnp.int32, (group, rows), 0) ^ z
    hits = jnp.where(live, owner, -1) == target
    upper = (
        lax.broadcasted_iota(jnp.int32, (rows, rows), 0) <= lax.broadcasted_iota(jnp.int32, (rows, rows), 1)
    )
    rank = jnp.dot(
        jnp.where(hits, 1.0, 0.0).astype(BF), jnp.where(upper, 1.0, 0.0).astype(BF), preferred_element_type=F32
    )
    slot = jnp.where(hits, rank - 1.0, -1.0).astype(jnp.int32)
    place = lax.broadcasted_iota(jnp.int32, (cap, rows), 0)
    select = [jnp.where(slot[d : d + 1] == place, 1.0, 0.0).astype(BF) for d in range(owners)]
    if labelled:
        tag = jnp.where(live, fine_ref[...] * COLS + mid - owner * COLS + 1, 0)
        line = lax.broadcasted_iota(jnp.int32, (LABEL_ROWS, rows), 0)
        digits = jnp.where(line == 0, tag // 256, jnp.where(line == 1, tag % 256, 0)).astype(F32).astype(BF)
    for e in range(subs):
        at = pl.multiple_of((s ^ e) * half + start, 128)
        block = traces_ref[:, pl.ds(at, width)]
        for d in range(owners):
            out = outs[e * owners + d]
            out[0:cap, :] = jnp.dot(select[d], block, preferred_element_type=F32).astype(BF)
            if labelled:
                out[cap : cap + LABEL_ROWS, :] = jnp.zeros((LABEL_ROWS, width), BF)
                out[cap : cap + LABEL_ROWS, 0:cap] = lax.dot_general(
                    digits, select[d], (((1,), (1,)), ((), ())), preferred_element_type=F32
                ).astype(BF)


def pack(plan, live_count, mid_bin, fine_class, records):
    owners, subs, cap, start, width, labelled = plan
    rows = cap + (LABEL_ROWS if labelled else 0)
    return pl.pallas_call(
        functools.partial(pack_kernel, plan),
        out_shape=[jax.ShapeDtypeStruct((rows, width), BF)] * (owners * subs),
        in_specs=[smem(), vmem(), vmem(), vmem()],
        out_specs=[vmem()] * (owners * subs),
        compiler_params=params(24),
        name="pack",
    )(live_count, mid_bin, fine_class, records)


def apply_blocks(first, blocks, stacked_ref, index_ref, ops_ref, acc_ref):
    fine, depth, taps = index_ref.shape
    width = ops_ref.shape[-1]
    for f in range(fine):
        for d in range(depth):
            for k in range(taps):
                at = index_ref[f, d, k] - first

                @pl.when((at >= 0) & (at < blocks))
                def _(f=f, d=d, k=k, at=at):
                    column = pl.multiple_of(at * width, width)
                    acc_ref[:, d * width : (d + 1) * width] += lax.dot_general(
                        stacked_ref[f * COLS : (f + 1) * COLS, pl.ds(column, width)],
                        ops_ref[f, d, k],
                        (((1,), (1,)), ((), ())),
                        preferred_element_type=F32,
                    )


def stack_kernel(cap, labelled, count, *refs):
    label_in = None if labelled else refs[0]
    given = refs[0 if labelled else 1 :][:count]
    stacked_ref = refs[count + (0 if labelled else 1)]
    scratch = refs[-1]
    if labelled:
        label_out = refs[count + 1]
        pieces = []
        for ref in given:
            digits = ref[cap : cap + LABEL_ROWS, 0:cap].astype(F32)
            pieces.append(256.0 * digits[0:1] + digits[1:2] - 1.0)
        label = jnp.concatenate(pieces, axis=1)
        label_out[...] = jnp.broadcast_to(label, label_out.shape)
    else:
        label = label_in[0:1, :]
    for i, ref in enumerate(given):
        scratch[i * cap : (i + 1) * cap, :] = ref[0:cap, :]
    segments = FINE * COLS

    def tile(t, carry):
        base = pl.multiple_of(t * TILE, TILE)
        line = (lax.broadcasted_iota(jnp.int32, (TILE, 1), 0) + base).astype(F32)
        chosen = jnp.where(label == line, 1.0, 0.0).astype(BF)
        stacked_ref[pl.ds(base, TILE), :] = jnp.dot(
            chosen, scratch[...], preferred_element_type=F32
        ).astype(BF)
        return carry

    lax.fori_loop(0, segments // TILE, tile, 0)


def stack(cap, label, given):
    width = given[0].shape[1]
    labelled = label is None
    slots = cap * len(given)
    out_shape = [jax.ShapeDtypeStruct((FINE * COLS, width), BF)]
    if labelled:
        out_shape.append(jax.ShapeDtypeStruct((8, slots), F32))
    operands = list(given) if labelled else [label, *given]
    return pl.pallas_call(
        functools.partial(stack_kernel, cap, labelled, len(given)),
        out_shape=out_shape,
        in_specs=[vmem()] * len(operands),
        out_specs=[vmem()] * len(out_shape),
        scratch_shapes=[pltpu.VMEM((slots, width), BF)],
        compiler_params=params(24),
        name="stack",
    )(*operands)


def operate_kernel(plan, index_ref, ops_ref, *refs):
    opening, closing, parts = plan
    refs = list(refs)
    acc_in = None if opening else refs.pop(0)
    given = refs[: len(parts)]
    outs = refs[len(parts) :]
    acc = outs[0]
    if opening:
        acc[...] = jnp.zeros_like(acc)
    else:
        acc[...] = acc_in[...]
    s = lax.axis_index("sub")
    width = ops_ref.shape[-1]
    for (other, half, start), ref in zip(parts, given):
        first = ((s ^ other) * half + start) // width
        apply_blocks(first, ref.shape[1] // width, ref, index_ref, ops_ref, acc)
    if closing:
        own, sent = outs[0], outs[1:]
        share = own.shape[0] // closing
        x = lax.axis_index("off")
        for k, ref in enumerate(sent):
            at = pl.multiple_of((x ^ (k + 1)) * share, share)
            ref[...] = own[pl.ds(at, share), :].astype(BF)


def operate(plan, index, ops, acc, given):
    opening, closing, parts = plan
    depth, width = ops.shape[1], ops.shape[-1]
    out_shape = [jax.ShapeDtypeStruct((COLS, depth * width), F32)]
    if closing:
        out_shape += [jax.ShapeDtypeStruct((COLS // closing, depth * width), BF)] * (closing - 1)
    operands = [index, ops] + ([] if opening else [acc]) + list(given)
    return pl.pallas_call(
        functools.partial(operate_kernel, plan),
        out_shape=out_shape,
        in_specs=[smem()] + [vmem()] * (len(operands) - 1),
        out_specs=[vmem()] * len(out_shape),
        input_output_aliases={} if opening else {2: 0},
        compiler_params=params(24),
        name="operate",
    )(*operands)


def swap(x, axis, mask):
    return lax.ppermute(x, axis, [(i, i ^ mask) for i in range(lax.axis_size(axis))])


def local(traces, mid_bin, live_count, fine_class, operator, block_index):
    records = traces[0]
    samples = records.shape[1]
    owners, subs, offs = (lax.axis_size(a) for a in ("bin", "sub", "off"))
    cap = 3 * records.shape[0] // (2 * owners)
    half = samples // subs
    ops = operator[0, :, 0]
    index = block_index[0, :, 0]
    cuts = ((0, half * 3 // 4), (half * 3 // 4, half // 4))

    def move(x, d, e):
        if d == 0 and e == 0:
            return x
        pairs = [
            (i * subs + j, (i ^ d) * subs + (j ^ e)) for i in range(owners) for j in range(subs)
        ]
        return lax.ppermute(x, ("bin", "sub"), pairs)

    arrived = []
    order = sorted(range(owners), key=lambda d: -d)
    for c, (start, width) in enumerate(cuts):
        packed = pack((owners, subs, cap, start, width, c == 0), live_count, mid_bin, fine_class, records)
        got = [None] * (owners * subs)
        for d in order:
            for e in range(subs):
                got[e * owners + d] = move(packed[e * owners + d], d, e)
        arrived.append(got)

    stacked0, label = stack(cap, None, arrived[0])
    other0 = swap(stacked0, "sub", 1)
    (acc,) = operate((True, 0, ((0, half, cuts[0][0]),)), index, ops, None, [stacked0])
    (acc,) = operate((False, 0, ((1, half, cuts[0][0]),)), index, ops, acc, [other0])
    (stacked1,) = stack(cap, label, arrived[1])
    other1 = swap(stacked1, "sub", 1)
    (acc,) = operate((False, 0, ((0, half, cuts[1][0]),)), index, ops, acc, [stacked1])
    acc, *sent = operate((False, offs, ((1, half, cuts[1][0]),)), index, ops, acc, [other1])
    share = COLS // offs
    total = lax.dynamic_slice_in_dim(acc, lax.axis_index("off") * share, share, axis=0)
    for k, piece in enumerate(sent):
        total = total + swap(piece, "off", k + 1).astype(F32)
    return total


def solution(mesh):
    placed = (
        P(("grp", "off"), ("bin", "sub"), None),
        P(("grp", "off"), ("bin", "sub")),
        P(("grp", "off"), ("bin", "sub")),
        P(("grp", "off"), ("bin", "sub")),
        P(("grp", "off"), None, "bin", "sub", None, None, None),
        P(("grp", "off"), None, "bin", "sub", None),
    )
    return jax.shard_map(
        local,
        mesh=mesh,
        in_specs=placed,
        out_specs=P(("grp", "bin", "off"), "sub"),
        check_vma=False,
    )
```

```python
import functools

import jax
import jax.numpy as jnp
from jax import lax
from jax.experimental import pallas as pl
from jax.experimental.pallas import tpu as pltpu
from jax.sharding import PartitionSpec as P

FINE = 2
COLS = 512
LINES = 16
TILE = 256
BF = jnp.bfloat16
F32 = jnp.float32
MIB = 1 << 20


def params(mib):
    return pltpu.CompilerParams(vmem_limit_bytes=mib * MIB)


def vmem():
    return pl.BlockSpec(memory_space=pltpu.VMEM)


def smem():
    return pl.BlockSpec(memory_space=pltpu.SMEM)


def call(body, out_shape, operands, scalars, name, mib=24, scratch=(), flops=0, after=()):
    moved = sum(a.size * a.dtype.itemsize for a in (*operands, *out_shape))
    count, late = len(operands), len(after)

    def run(*refs):
        body(*refs[:count], *refs[count + late :])

    return pl.pallas_call(
        run,
        out_shape=list(out_shape),
        in_specs=[smem()] * scalars + [vmem()] * (count - scalars + late),
        out_specs=[vmem()] * len(out_shape),
        scratch_shapes=list(scratch),
        compiler_params=params(mib),
        cost_estimate=pl.CostEstimate(flops=flops, bytes_accessed=moved, transcendentals=0),
        name=name,
    )(*operands, *(corner(a) for a in after))


def corner(a):
    return a[:LINES, :128]


def gate(given, after):
    return pl.pallas_call(
        lambda *refs: None,
        out_shape=[jax.ShapeDtypeStruct(a.shape, a.dtype) for a in given],
        in_specs=[vmem()] * (len(given) + len(after)),
        out_specs=[vmem()] * len(given),
        input_output_aliases={i: i for i in range(len(given))},
        compiler_params=params(4),
        cost_estimate=pl.CostEstimate(flops=0, bytes_accessed=0, transcendentals=0),
        name="gate",
    )(*given, *(corner(a) for a in after))


def shape(rows, columns, kind=BF):
    return jax.ShapeDtypeStruct((rows, columns), kind)


def one_hot(mask):
    return jnp.where(mask, 1.0, 0.0).astype(BF)


def running_count(mask_rows):
    rows = mask_rows.shape[1]
    upper = lax.broadcasted_iota(jnp.int32, (rows, rows), 0) <= lax.broadcasted_iota(jnp.int32, (rows, rows), 1)
    return jnp.dot(one_hot(mask_rows), one_hot(upper), preferred_element_type=F32)


def choose(position, slots):
    place = lax.broadcasted_iota(jnp.int32, (slots, position.shape[1]), 0).astype(F32)
    return one_hot(position == place)


def tag_digits(live, owner, mid, fine, lines=LINES):
    tag = jnp.where(live, fine * COLS + mid - owner * COLS + 1, 0)
    line = lax.broadcasted_iota(jnp.int32, (lines, tag.shape[1]), 0)
    return jnp.where(line == 0, tag // 256, jnp.where(line == 1, tag % 256, 0)).astype(F32).astype(BF)


def across(digits, chosen):
    return lax.dot_general(digits, chosen, (((1,), (1,)), ((), ())), preferred_element_type=F32)


def tag_of(lines):
    lines = lines.astype(F32)
    return 256.0 * lines[0:1] + lines[1:2] - 1.0


def full_pack_kernel(owners, cap, live_ref, mid_ref, fine_ref, traces_ref, *outs):
    z = lax.axis_index("bin")
    rows, samples = traces_ref.shape
    live = lax.broadcasted_iota(jnp.int32, (1, rows), 1) < live_ref[0, 0]
    mid = mid_ref[...]
    owner = mid // COLS
    target = lax.broadcasted_iota(jnp.int32, (max(owners, 16), rows), 0) ^ z
    hits = jnp.where(live, owner, -1) == target
    slot = jnp.where(hits, running_count(hits) - 1.0, -1.0)
    digits = tag_digits(live, owner, mid, fine_ref[...])
    for d in range(owners):
        select = choose(slot[d : d + 1], cap)
        outs[d][0:cap, :] = jnp.dot(select, traces_ref[...], preferred_element_type=F32).astype(BF)
        outs[d][cap : cap + LINES, :] = jnp.zeros((LINES, samples), BF)
        outs[d][cap : cap + LINES, 0:cap] = across(digits, select).astype(BF)


def full_stack_kernel(cap, *refs):
    *given, stacked_ref, rows_ref = refs
    label = jnp.concatenate([tag_of(ref[cap : cap + LINES, 0:cap]) for ref in given], axis=1)
    for i, ref in enumerate(given):
        rows_ref[i * cap : (i + 1) * cap, :] = ref[0:cap, :]

    def tile(t, carry):
        base = pl.multiple_of(t * TILE, TILE)
        line = (lax.broadcasted_iota(jnp.int32, (TILE, 1), 0) + base).astype(F32)
        stacked_ref[pl.ds(base, TILE), :] = jnp.dot(
            one_hot(label == line), rows_ref[...], preferred_element_type=F32
        ).astype(BF)
        return carry

    lax.fori_loop(0, FINE * COLS // TILE, tile, 0)


def image_terms(d, index_ref, ops_ref, stacked_ref):
    fine, _, taps = index_ref.shape
    width = ops_ref.shape[-1]
    columns = stacked_ref.shape[0] // fine
    picked, weights = [], []
    for f in range(fine):
        for k in range(taps):
            at = pl.multiple_of(index_ref[f, d, k] * width, width)
            picked.append(stacked_ref[f * columns : (f + 1) * columns, pl.ds(at, width)])
            weights.append(ops_ref[f, d, k])
    return lax.dot_general(
        jnp.concatenate(picked, axis=1),
        jnp.concatenate(weights, axis=1),
        (((1,), (1,)), ((), ())),
        preferred_element_type=F32,
    )


def operate_kernel(index_ref, ops_ref, stacked_ref, out_ref):
    width = ops_ref.shape[-1]
    for d in range(index_ref.shape[1]):
        terms = image_terms(d, index_ref, ops_ref, stacked_ref)
        out_ref[0 : terms.shape[0], d * width : (d + 1) * width] = terms.astype(out_ref.dtype)


def operate(index, ops, stacked, kind):
    columns, depth = stacked.shape[0] // FINE, ops.shape[1] * ops.shape[-1]
    (out,) = call(
        operate_kernel,
        [shape(columns, depth, kind)],
        [index, ops, stacked],
        1,
        "operate",
        flops=2 * columns * ops.size,
    )
    return out


def send_kernel(index_ref, ops_ref, stacked_ref, *outs):
    width = ops_ref.shape[-1]
    each = outs[0].shape[1]
    for d in range(index_ref.shape[1]):
        piece, at = outs[d * width // each], d * width % each
        piece[:, at : at + width] = image_terms(d, index_ref, ops_ref, stacked_ref).astype(BF)


def finish_kernel(index_ref, ops_ref, stacked_ref, *refs):
    *came, out_ref = refs
    width = ops_ref.shape[-1]
    each = came[0].shape[1]
    for d in range(index_ref.shape[1]):
        piece, at = came[d * width // each], d * width % each
        more = piece[:, at : at + width].astype(F32)
        out_ref[:, d * width : (d + 1) * width] = image_terms(d, index_ref, ops_ref, stacked_ref) + more


def swap(x, axis, mask):
    return lax.ppermute(x, axis, [(i, i ^ mask) for i in range(lax.axis_size(axis))])


def static_path(cap, records, mid_bin, live_count, fine_class, ops, index):
    owners, subs, offs = (lax.axis_size(a) for a in ("bin", "sub", "off"))
    samples = records.shape[1]
    packed = call(
        functools.partial(full_pack_kernel, owners, cap),
        [shape(cap + LINES, samples)] * owners,
        [live_count, mid_bin, fine_class, records],
        1,
        "full_pack",
    )
    arrived = [packed[0]] + [swap(packed[d], "bin", d) for d in range(1, owners)]
    arrived += [swap(a, "sub", e) for e in range(1, subs) for a in arrived]
    (stacked,) = call(
        functools.partial(full_stack_kernel, cap),
        [shape(FINE * COLS, samples)],
        arrived,
        0,
        "full_stack",
        mib=32,
        scratch=[pltpu.VMEM((cap * len(arrived), samples), BF)],
    )
    terms = operate(index, ops, stacked, F32)
    share = COLS // offs
    x = lax.axis_index("off")
    total = lax.dynamic_slice_in_dim(terms, x * share, share, axis=0)
    for k in range(1, offs):
        total = total + swap(lax.dynamic_slice_in_dim(terms, (x ^ k) * share, share, axis=0), "off", k)
    return total


class Slots:
    def __init__(self, cap):
        self.cap = cap
        self.each = 2 * cap // 3
        self.spare = cap - self.each
        self.front = 5 * cap // 12
        self.back = self.each - self.front
        self.near_front = 2 * cap // 3
        self.near_back = cap - self.near_front
        self.first = 2 * self.spare + 2 * self.front + self.near_front
        self.second = 2 * self.back + self.near_back


def positions(q, live_ref, mid_ref):
    rows = mid_ref.shape[1]
    z, x = lax.axis_index("bin"), lax.axis_index("off")
    live = lax.broadcasted_iota(jnp.int32, (1, rows), 1) < live_ref[0, 0]
    mid = mid_ref[...]
    owner = mid // COLS
    share = COLS // 2
    kept = jnp.where((mid - owner * COLS) // share == x, 1, 0)
    kind = jnp.where(live, (owner ^ z) * 2 + kept, -1)
    hits = lax.broadcasted_iota(jnp.int32, (16, rows), 0) == kind
    rank = running_count(hits)
    seat = jnp.where(hits, rank - 1.0, -1.0)
    place, late = [], []
    for d in range(4):
        first, second = seat[2 * d : 2 * d + 1], seat[2 * d + 1 : 2 * d + 2]
        if d < 2:
            place.append(jnp.where(first >= 0, first, jnp.where(second >= 0, q.cap - 1.0 - second, -1.0)))
            continue
        taken = jnp.minimum(rank[2 * d : 2 * d + 1, rows - 1 : rows], float(q.front))
        mirrored = q.each - 1.0 - second
        in_front = (first >= 0) & (first < q.front)
        in_rest = (second >= 0) & (mirrored >= taken)
        place.append(jnp.where(in_front, first, jnp.where(in_rest, mirrored, -1.0)))
        late.append(((first >= q.front) | ((second >= 0) & (mirrored < taken))))
    line = lax.broadcasted_iota(jnp.int32, (16, rows), 0)
    either = jnp.where(late[0] | late[1], 1, 0)
    after = running_count((line == 0) & (either == 1))[0:1]
    spare = jnp.where(either == 1, after - 1.0, -1.0)
    excess = jnp.maximum(after[:, rows - 1 : rows] - q.spare, rank[2:3, rows - 1 : rows] - q.near_front)
    return live, mid, owner, place, spare, late, excess


def lay(ref, rows, tags):
    size = rows.shape[0]
    ref[0:size, :] = rows
    ref[size : size + LINES, :] = jnp.zeros((LINES, ref.shape[1]), BF)
    ref[size : size + LINES, 0 : tags.shape[1]] = tags.astype(BF)


def pack_spare_kernel(q, live_ref, mid_ref, fine_ref, traces_ref, spare_ref, own_ref, flag_ref):
    live, mid, owner, place, spare, late, excess = positions(q, live_ref, mid_ref)
    digits = tag_digits(live, owner, mid, fine_ref[...])
    extra = [choose(jnp.where(late[i], spare, -1.0), q.spare) for i in range(2)]
    tags = [across(digits, jnp.concatenate([choose(place[d], q.each), extra[d - 2]], axis=0)) for d in (2, 3)]
    crossing = jnp.concatenate([tags[0][0:4], tags[1][0:4], jnp.zeros((LINES - 8, q.cap), F32)], axis=0)
    own = choose(place[0], q.cap)
    chosen = jnp.concatenate([extra[0] + extra[1], own], axis=0)
    rows = jnp.dot(chosen, traces_ref[...], preferred_element_type=F32).astype(BF)
    lay(spare_ref, rows[: q.spare], crossing)
    lay(own_ref, rows[q.spare :], across(digits, own))
    flag_ref[...] = jnp.broadcast_to(jnp.where(excess > 0.0, 1.0, 0.0), flag_ref.shape)


def pack_rest_kernel(
    q, live_ref, mid_ref, fine_ref, traces_ref, cross2_ref, cross3_ref, near_ref, back2_ref, back3_ref, near_back_ref
):
    live, mid, owner, place, _, _, _ = positions(q, live_ref, mid_ref)
    digits = tag_digits(live, owner, mid, fine_ref[...])
    near = choose(place[1], q.cap)
    chosen = jnp.concatenate([choose(place[2], q.each), choose(place[3], q.each), near], axis=0)
    rows = jnp.dot(chosen, traces_ref[...], preferred_element_type=F32).astype(BF)
    cross2_ref[...] = rows[: q.front]
    back2_ref[...] = rows[q.front : q.each]
    cross3_ref[...] = rows[q.each : q.each + q.front]
    back3_ref[...] = rows[q.each + q.front : 2 * q.each]
    at = 2 * q.each + q.near_front
    lay(near_ref, rows[2 * q.each : at], across(digits, near))
    near_back_ref[...] = rows[at:]


def relay_kernel(q, spare_ref, flag_ref, out_ref):
    out_ref[0 : q.spare, :] = spare_ref[0 : q.spare, :]
    lines = spare_ref[q.spare : q.spare + LINES, :]
    row = lax.broadcasted_iota(jnp.int32, lines.shape, 0)
    out_ref[q.spare : q.spare + LINES, :] = jnp.where(row == 3, flag_ref[0:1, 0:1].astype(BF), lines)


def gather_kernel(
    q, spare_ref, cross2_ref, cross3_ref, near_ref, relay_ref, own_flag_ref, rows_ref, flag_ref
):
    at = 0
    for ref, size in (
        (spare_ref, q.spare),
        (cross2_ref, q.front),
        (cross3_ref, q.front),
        (near_ref, q.near_front),
        (relay_ref, q.spare),
    ):
        rows_ref[at : at + size, :] = ref[0:size, :]
        at += size
    cross2, cross3, near = (
        ref[size : size + LINES, 0 : q.cap].astype(F32)
        for ref, size in ((spare_ref, q.spare), (relay_ref, q.spare), (near_ref, q.near_front))
    )
    flag_ref[...] = jnp.maximum(own_flag_ref[...], jnp.broadcast_to(cross3[3:4, 0:128], flag_ref.shape))
    cross2, cross3, near = cross2[0:2], cross3[4:6], near[0:2]
    tags = jnp.concatenate(
        [
            cross2[:, q.each :],
            cross2[:, : q.front],
            cross3[:, : q.front],
            near[:, : q.near_front],
            cross3[:, q.each :],
            cross2[:, q.front : q.each],
            cross3[:, q.front : q.each],
            near[:, q.near_front :],
        ],
        axis=1,
    )
    tags = jnp.concatenate([tags, jnp.zeros((LINES - 2, tags.shape[1]), F32)], axis=0)
    rows_ref[at : at + LINES, :] = jnp.zeros((LINES, rows_ref.shape[1]), BF)
    rows_ref[at : at + LINES, 0 : tags.shape[1]] = tags.astype(BF)


def segment_line(f, part):
    base = f * COLS + part * (COLS // 2)
    return (lax.broadcasted_iota(jnp.int32, (COLS // 2, 1), 0) + base).astype(F32)


def stack_into(out_ref, given, part):
    labels = []
    for ref in given:
        count = ref.shape[0] - LINES
        labels.append(tag_of(ref[count : count + LINES, 0:count]))
    share = COLS // 2
    for f in range(FINE):
        line = segment_line(f, part)
        out_ref[f * share : (f + 1) * share, :] = sum(
            jnp.dot(one_hot(label == line), ref[0 : label.shape[1], :], preferred_element_type=F32)
            for label, ref in zip(labels, given)
        ).astype(out_ref.dtype)


def stack_sent_kernel(q, *refs):
    *given, sent_ref, tags_ref = refs
    tags = [tag_of(ref[q.first : q.first + LINES, q.first : q.first + q.second]) for ref in given[:2]]
    tags_ref[...] = jnp.broadcast_to(jnp.concatenate(tags, axis=1), tags_ref.shape)
    stack_into(sent_ref, given, 1 - lax.axis_index("off"))


def stack_kept_kernel(*refs):
    *given, kept_ref = refs
    stack_into(kept_ref, given, lax.axis_index("off"))


def join_kernel(*refs):
    *given, out_ref = refs
    at = 0
    for ref in given:
        out_ref[at : at + ref.shape[0], :] = ref[...]
        at += ref.shape[0]


def stack_second_kernel(q, tags_ref, kept_ref, own_ref, other_ref, out_ref, rows_ref):
    x = lax.axis_index("off")
    rows_ref[: q.second, :] = own_ref[...]
    rows_ref[q.second :, :] = other_ref[...]
    label = tags_ref[0:1, :]
    share = COLS // 2
    for f in range(FINE):
        span = slice(f * share, (f + 1) * share)
        more = jnp.dot(one_hot(label == segment_line(f, x)), rows_ref[...], preferred_element_type=F32)
        out_ref[span, :] = (kept_ref[span, :] + more).astype(BF)


def short_path(cap, records, mid_bin, live_count, fine_class, ops, index):
    q = Slots(cap)
    samples = records.shape[1]
    share, depth = COLS // 2, ops.shape[1] * ops.shape[-1]
    packed, own, flag = call(
        functools.partial(pack_spare_kernel, q),
        [shape(q.spare + LINES, samples), shape(q.cap + LINES, samples), shape(8, 128, F32)],
        [live_count, mid_bin, fine_class, records],
        1,
        "pack_spare",
        flops=2 * (q.spare + q.cap) * records.size,
    )
    spare, own_other = swap(packed, "bin", 2), swap(own, "sub", 1)
    cross2, cross3, near, back2, back3, near_back = call(
        functools.partial(pack_rest_kernel, q),
        [shape(q.front, samples)] * 2
        + [shape(q.near_front + LINES, samples)]
        + [shape(q.back, samples)] * 2
        + [shape(q.near_back, samples)],
        [live_count, mid_bin, fine_class, records],
        1,
        "pack_rest",
        flops=2 * (2 * q.each + q.cap) * records.size,
        after=[packed],
    )
    cross2, cross3, near = swap(cross2, "bin", 2), swap(cross3, "bin", 3), swap(near, "bin", 1)
    for axis in ("sub", "off", "grp"):
        mask = 1
        while mask < lax.axis_size(axis):
            flag = jnp.maximum(flag, swap(flag, axis, mask))
            mask *= 2
    (relay,) = call(
        functools.partial(relay_kernel, q), [shape(q.spare + LINES, samples)], [spare, flag], 0, "relay"
    )
    relay = swap(relay, "bin", 1)
    back2, back3, near_back = gate([back2, back3, near_back], [cross3])
    rows, flag = call(
        functools.partial(gather_kernel, q),
        [shape(q.first + LINES, samples), shape(8, 128, F32)],
        [spare, cross2, cross3, near, relay, flag],
        0,
        "gather",
        after=[back2],
    )
    back2, back3, near_back = swap(back2, "bin", 2), swap(back3, "bin", 3), swap(near_back, "bin", 1)
    given = [rows, swap(rows, "sub", 1), own, own_other]
    flops = 2 * FINE * COLS * (q.first + q.cap) * samples
    sent, tags = call(
        functools.partial(stack_sent_kernel, q),
        [shape(FINE * share, samples), shape(8, 2 * q.second, F32)],
        given,
        0,
        "stack_sent",
        flops=flops,
    )
    terms = call(
        send_kernel,
        [shape(share, depth // 2)] * 2,
        [index, ops, sent],
        1,
        "operate",
        flops=2 * share * ops.size,
    )
    came = [swap(piece, "off", 1) for piece in terms]
    (kept,) = call(
        stack_kept_kernel,
        [shape(FINE * share, samples, F32)],
        given,
        0,
        "stack_kept",
        flops=flops,
        after=[terms[0]],
    )
    flag = jnp.maximum(flag, swap(flag, "bin", 2))
    (late,) = call(
        join_kernel,
        [shape(q.second, samples)],
        [back2, back3, near_back],
        0,
        "join",
        after=[kept, *came, flag],
    )
    (stacked,) = call(
        functools.partial(stack_second_kernel, q),
        [shape(FINE * share, samples)],
        [tags, kept, late, swap(late, "sub", 1)],
        0,
        "stack_second",
        scratch=[pltpu.VMEM((2 * q.second, samples), BF)],
        flops=2 * FINE * COLS * q.second * samples,
    )
    (image,) = call(
        finish_kernel,
        [shape(share, depth, F32)],
        [index, ops, stacked, *came],
        1,
        "finish",
        flops=2 * share * ops.size,
    )
    given = (records, mid_bin, live_count, fine_class, ops, index)
    return lax.cond(flag[0, 0] > 0.0, lambda image, *a: static_path(cap, *a), lambda image, *a: image, image, *given)


def local(traces, mid_bin, live_count, fine_class, operator, block_index):
    records = traces[0]
    owners, offs = lax.axis_size("bin"), lax.axis_size("off")
    cap = 3 * records.shape[0] // (2 * owners)
    path = short_path if owners == 4 and offs == 2 else static_path
    return path(cap, records, mid_bin, live_count, fine_class, operator[0, :, 0], block_index[0, :, 0])


def solution(mesh):
    placed = (
        P(("grp", "off"), ("bin", "sub"), None),
        P(("grp", "off"), ("bin", "sub")),
        P(("grp", "off"), ("bin", "sub")),
        P(("grp", "off"), ("bin", "sub")),
        P(("grp", "off"), None, "bin", "sub", None, None, None),
        P(("grp", "off"), None, "bin", "sub", None),
    )
    return jax.shard_map(
        local,
        mesh=mesh,
        in_specs=placed,
        out_specs=P(("grp", "bin", "off"), "sub"),
        check_vma=False,
    )
```

```python
import functools

import jax
import jax.numpy as jnp
from jax import lax
from jax.experimental import pallas as pl
from jax.experimental.pallas import tpu as pltpu
from jax.sharding import PartitionSpec as P

FINE = 2
COLS = 512
LINES = 16
TILE = 256
BF = jnp.bfloat16
F32 = jnp.float32
MIB = 1 << 20


def params(mib):
    return pltpu.CompilerParams(vmem_limit_bytes=mib * MIB)


def vmem():
    return pl.BlockSpec(memory_space=pltpu.VMEM)


def smem():
    return pl.BlockSpec(memory_space=pltpu.SMEM)


def call(body, out_shape, operands, scalars, name, mib=24, scratch=(), flops=0, after=()):
    moved = sum(a.size * a.dtype.itemsize for a in (*operands, *out_shape))
    count, late = len(operands), len(after)

    def run(*refs):
        body(*refs[:count], *refs[count + late :])

    return pl.pallas_call(
        run,
        out_shape=list(out_shape),
        in_specs=[smem()] * scalars + [vmem()] * (count - scalars + late),
        out_specs=[vmem()] * len(out_shape),
        scratch_shapes=list(scratch),
        compiler_params=params(mib),
        cost_estimate=pl.CostEstimate(flops=flops, bytes_accessed=moved, transcendentals=0),
        name=name,
    )(*operands, *(corner(a) for a in after))


def corner(a):
    return a[:LINES, :128]


def gate(given, after):
    return pl.pallas_call(
        lambda *refs: None,
        out_shape=[jax.ShapeDtypeStruct(a.shape, a.dtype) for a in given],
        in_specs=[vmem()] * (len(given) + len(after)),
        out_specs=[vmem()] * len(given),
        input_output_aliases={i: i for i in range(len(given))},
        compiler_params=params(4),
        cost_estimate=pl.CostEstimate(flops=0, bytes_accessed=0, transcendentals=0),
        name="gate",
    )(*given, *(corner(a) for a in after))


def shape(rows, columns, kind=BF):
    return jax.ShapeDtypeStruct((rows, columns), kind)


def one_hot(mask):
    return jnp.where(mask, 1.0, 0.0).astype(BF)


def running_count(mask_rows):
    rows = mask_rows.shape[1]
    upper = lax.broadcasted_iota(jnp.int32, (rows, rows), 0) <= lax.broadcasted_iota(jnp.int32, (rows, rows), 1)
    return jnp.dot(one_hot(mask_rows), one_hot(upper), preferred_element_type=F32)


def choose(position, slots):
    place = lax.broadcasted_iota(jnp.int32, (slots, position.shape[1]), 0).astype(F32)
    return one_hot(position == place)


def tag_digits(live, owner, mid, fine, lines=LINES):
    tag = jnp.where(live, fine * COLS + mid - owner * COLS + 1, 0)
    line = lax.broadcasted_iota(jnp.int32, (lines, tag.shape[1]), 0)
    return jnp.where(line == 0, tag // 256, jnp.where(line == 1, tag % 256, 0)).astype(F32).astype(BF)


def across(digits, chosen):
    return lax.dot_general(digits, chosen, (((1,), (1,)), ((), ())), preferred_element_type=F32)


def tag_of(lines):
    lines = lines.astype(F32)
    return 256.0 * lines[0:1] + lines[1:2] - 1.0


def full_pack_kernel(owners, cap, live_ref, mid_ref, fine_ref, traces_ref, *outs):
    z = lax.axis_index("bin")
    rows, samples = traces_ref.shape
    live = lax.broadcasted_iota(jnp.int32, (1, rows), 1) < live_ref[0, 0]
    mid = mid_ref[...]
    owner = mid // COLS
    target = lax.broadcasted_iota(jnp.int32, (max(owners, 16), rows), 0) ^ z
    hits = jnp.where(live, owner, -1) == target
    slot = jnp.where(hits, running_count(hits) - 1.0, -1.0)
    digits = tag_digits(live, owner, mid, fine_ref[...])
    for d in range(owners):
        select = choose(slot[d : d + 1], cap)
        outs[d][0:cap, :] = jnp.dot(select, traces_ref[...], preferred_element_type=F32).astype(BF)
        outs[d][cap : cap + LINES, :] = jnp.zeros((LINES, samples), BF)
        outs[d][cap : cap + LINES, 0:cap] = across(digits, select).astype(BF)


def full_stack_kernel(cap, *refs):
    *given, stacked_ref, rows_ref = refs
    label = jnp.concatenate([tag_of(ref[cap : cap + LINES, 0:cap]) for ref in given], axis=1)
    for i, ref in enumerate(given):
        rows_ref[i * cap : (i + 1) * cap, :] = ref[0:cap, :]

    def tile(t, carry):
        base = pl.multiple_of(t * TILE, TILE)
        line = (lax.broadcasted_iota(jnp.int32, (TILE, 1), 0) + base).astype(F32)
        stacked_ref[pl.ds(base, TILE), :] = jnp.dot(
            one_hot(label == line), rows_ref[...], preferred_element_type=F32
        ).astype(BF)
        return carry

    lax.fori_loop(0, FINE * COLS // TILE, tile, 0)


def image_terms(d, index_ref, ops_ref, stacked_ref):
    fine, _, taps = index_ref.shape
    width = ops_ref.shape[-1]
    columns = stacked_ref.shape[0] // fine
    picked, weights = [], []
    for f in range(fine):
        for k in range(taps):
            at = pl.multiple_of(index_ref[f, d, k] * width, width)
            picked.append(stacked_ref[f * columns : (f + 1) * columns, pl.ds(at, width)])
            weights.append(ops_ref[f, d, k])
    return lax.dot_general(
        jnp.concatenate(picked, axis=1),
        jnp.concatenate(weights, axis=1),
        (((1,), (1,)), ((), ())),
        preferred_element_type=F32,
    )


def operate_kernel(index_ref, ops_ref, stacked_ref, out_ref):
    width = ops_ref.shape[-1]
    for d in range(index_ref.shape[1]):
        terms = image_terms(d, index_ref, ops_ref, stacked_ref)
        out_ref[0 : terms.shape[0], d * width : (d + 1) * width] = terms.astype(out_ref.dtype)


def operate(index, ops, stacked, kind):
    columns, depth = stacked.shape[0] // FINE, ops.shape[1] * ops.shape[-1]
    (out,) = call(
        operate_kernel,
        [shape(columns, depth, kind)],
        [index, ops, stacked],
        1,
        "operate",
        flops=2 * columns * ops.size,
    )
    return out


def send_kernel(index_ref, ops_ref, stacked_ref, *outs):
    width = ops_ref.shape[-1]
    each = outs[0].shape[1]
    for d in range(index_ref.shape[1]):
        piece, at = outs[d * width // each], d * width % each
        piece[:, at : at + width] = image_terms(d, index_ref, ops_ref, stacked_ref).astype(BF)


def finish_kernel(index_ref, ops_ref, stacked_ref, *refs):
    *came, out_ref = refs
    width = ops_ref.shape[-1]
    each = came[0].shape[1]
    for d in range(index_ref.shape[1]):
        piece, at = came[d * width // each], d * width % each
        more = piece[:, at : at + width].astype(F32)
        out_ref[:, d * width : (d + 1) * width] = image_terms(d, index_ref, ops_ref, stacked_ref) + more


def swap(x, axis, mask):
    return lax.ppermute(x, axis, [(i, i ^ mask) for i in range(lax.axis_size(axis))])


def static_path(cap, records, mid_bin, live_count, fine_class, ops, index):
    owners, subs, offs = (lax.axis_size(a) for a in ("bin", "sub", "off"))
    samples = records.shape[1]
    packed = call(
        functools.partial(full_pack_kernel, owners, cap),
        [shape(cap + LINES, samples)] * owners,
        [live_count, mid_bin, fine_class, records],
        1,
        "full_pack",
    )
    arrived = [packed[0]] + [swap(packed[d], "bin", d) for d in range(1, owners)]
    arrived += [swap(a, "sub", e) for e in range(1, subs) for a in arrived]
    (stacked,) = call(
        functools.partial(full_stack_kernel, cap),
        [shape(FINE * COLS, samples)],
        arrived,
        0,
        "full_stack",
        mib=32,
        scratch=[pltpu.VMEM((cap * len(arrived), samples), BF)],
    )
    terms = operate(index, ops, stacked, F32)
    share = COLS // offs
    x = lax.axis_index("off")
    total = lax.dynamic_slice_in_dim(terms, x * share, share, axis=0)
    for k in range(1, offs):
        total = total + swap(lax.dynamic_slice_in_dim(terms, (x ^ k) * share, share, axis=0), "off", k)
    return total


class Slots:
    def __init__(self, cap):
        self.cap = cap
        self.each = 2 * cap // 3
        self.spare = cap - self.each
        self.front = 5 * cap // 12
        self.back = self.each - self.front
        self.near_front = 2 * cap // 3
        self.near_back = cap - self.near_front
        self.first = 2 * self.spare + 2 * self.front + self.near_front
        self.second = 2 * self.back + self.near_back


def positions(q, live_ref, mid_ref):
    rows = mid_ref.shape[1]
    z, x = lax.axis_index("bin"), lax.axis_index("off")
    live = lax.broadcasted_iota(jnp.int32, (1, rows), 1) < live_ref[0, 0]
    mid = mid_ref[...]
    owner = mid // COLS
    share = COLS // 2
    kept = jnp.where((mid - owner * COLS) // share == x, 1, 0)
    kind = jnp.where(live, (owner ^ z) * 2 + kept, -1)
    hits = lax.broadcasted_iota(jnp.int32, (16, rows), 0) == kind
    rank = running_count(hits)
    seat = jnp.where(hits, rank - 1.0, -1.0)
    place, late = [], []
    for d in range(4):
        first, second = seat[2 * d : 2 * d + 1], seat[2 * d + 1 : 2 * d + 2]
        if d < 2:
            place.append(jnp.where(first >= 0, first, jnp.where(second >= 0, q.cap - 1.0 - second, -1.0)))
            continue
        taken = jnp.minimum(rank[2 * d : 2 * d + 1, rows - 1 : rows], float(q.front))
        mirrored = q.each - 1.0 - second
        in_front = (first >= 0) & (first < q.front)
        in_rest = (second >= 0) & (mirrored >= taken)
        place.append(jnp.where(in_front, first, jnp.where(in_rest, mirrored, -1.0)))
        late.append(((first >= q.front) | ((second >= 0) & (mirrored < taken))))
    line = lax.broadcasted_iota(jnp.int32, (16, rows), 0)
    either = jnp.where(late[0] | late[1], 1, 0)
    after = running_count((line == 0) & (either == 1))[0:1]
    spare = jnp.where(either == 1, after - 1.0, -1.0)
    excess = jnp.maximum(after[:, rows - 1 : rows] - q.spare, rank[2:3, rows - 1 : rows] - q.near_front)
    return live, mid, owner, place, spare, late, excess


def lay(ref, rows, tags):
    size = rows.shape[0]
    ref[0:size, :] = rows
    ref[size : size + LINES, :] = jnp.zeros((LINES, ref.shape[1]), BF)
    ref[size : size + LINES, 0 : tags.shape[1]] = tags.astype(BF)


def pack_spare_kernel(
    q, live_ref, mid_hbm, fine_hbm, traces_ref, spare_ref, lines_ref, own_ref, flag_ref, held_ref, mid_ref, fine_ref, sems
):
    copies = [
        pltpu.make_async_copy(mid_hbm, mid_ref, sems.at[0]),
        pltpu.make_async_copy(fine_hbm, fine_ref, sems.at[1]),
    ]
    count = sems.shape[0] - 2
    step = held_ref.shape[0] // count
    for i in range(count):
        span = pl.ds(i * step, step)
        copies.append(pltpu.make_async_copy(traces_ref.at[span], held_ref.at[span], sems.at[i + 2]))
    for copy in copies:
        copy.start()
    for copy in copies[:2]:
        copy.wait()
    live, mid, owner, place, spare, late, excess = positions(q, live_ref, mid_ref)
    digits = tag_digits(live, owner, mid, fine_ref[...])
    extra = [choose(jnp.where(late[i], spare, -1.0), q.spare) for i in range(2)]
    tags = [across(digits, jnp.concatenate([choose(place[d], q.each), extra[d - 2]], axis=0)) for d in (2, 3)]
    crossing = jnp.concatenate([tags[0][0:4], tags[1][0:4], jnp.zeros((LINES - 8, q.cap), F32)], axis=0)
    own = choose(place[0], q.cap)
    chosen = jnp.concatenate([extra[0] + extra[1], own], axis=0)
    lines_ref[...] = jnp.zeros(lines_ref.shape, BF)
    lines_ref[:, 0 : q.cap] = crossing.astype(BF)
    for copy in copies[2:]:
        copy.wait()
    rows = jnp.dot(chosen, held_ref[...], preferred_element_type=F32).astype(BF)
    spare_ref[...] = rows[: q.spare]
    lay(own_ref, rows[q.spare :], across(digits, own))
    flag_ref[...] = jnp.broadcast_to(jnp.where(excess > 0.0, 1.0, 0.0), flag_ref.shape)


def pack_rest_kernel(
    q, live_ref, mid_ref, fine_ref, traces_ref, cross2_ref, cross3_ref, near_ref, back2_ref, back3_ref, near_back_ref
):
    live, mid, owner, place, _, _, _ = positions(q, live_ref, mid_ref)
    digits = tag_digits(live, owner, mid, fine_ref[...])
    near = choose(place[1], q.cap)
    chosen = jnp.concatenate([choose(place[2], q.each), choose(place[3], q.each), near], axis=0)
    rows = jnp.dot(chosen, traces_ref[...], preferred_element_type=F32).astype(BF)
    cross2_ref[...] = rows[: q.front]
    back2_ref[...] = rows[q.front : q.each]
    cross3_ref[...] = rows[q.each : q.each + q.front]
    back3_ref[...] = rows[q.each + q.front : 2 * q.each]
    at = 2 * q.each + q.near_front
    lay(near_ref, rows[2 * q.each : at], across(digits, near))
    near_back_ref[...] = rows[at:]


def relay_kernel(q, spare_ref, lines_ref, flag_ref, out_ref):
    out_ref[0 : q.spare, :] = spare_ref[...]
    row = lax.broadcasted_iota(jnp.int32, lines_ref.shape, 0)
    out_ref[q.spare : q.spare + LINES, :] = jnp.zeros((LINES, out_ref.shape[1]), BF)
    out_ref[q.spare : q.spare + LINES, 0 : lines_ref.shape[1]] = jnp.where(
        row == 3, flag_ref[0:1, 0:1].astype(BF), lines_ref[...]
    )


def gather_kernel(
    q, spare_ref, lines_ref, cross2_ref, cross3_ref, near_ref, relay_ref, own_flag_ref, rows_ref, flag_ref
):
    at = 0
    for ref, size in (
        (spare_ref, q.spare),
        (cross2_ref, q.front),
        (cross3_ref, q.front),
        (near_ref, q.near_front),
        (relay_ref, q.spare),
    ):
        rows_ref[at : at + size, :] = ref[0:size, :]
        at += size
    cross2, cross3, near = (
        ref[size : size + LINES, 0 : q.cap].astype(F32)
        for ref, size in ((lines_ref, 0), (relay_ref, q.spare), (near_ref, q.near_front))
    )
    flag_ref[...] = jnp.maximum(own_flag_ref[...], jnp.broadcast_to(cross3[3:4, 0:128], flag_ref.shape))
    cross2, cross3, near = cross2[0:2], cross3[4:6], near[0:2]
    tags = jnp.concatenate(
        [
            cross2[:, q.each :],
            cross2[:, : q.front],
            cross3[:, : q.front],
            near[:, : q.near_front],
            cross3[:, q.each :],
            cross2[:, q.front : q.each],
            cross3[:, q.front : q.each],
            near[:, q.near_front :],
        ],
        axis=1,
    )
    tags = jnp.concatenate([tags, jnp.zeros((LINES - 2, tags.shape[1]), F32)], axis=0)
    rows_ref[at : at + LINES, :] = jnp.zeros((LINES, rows_ref.shape[1]), BF)
    rows_ref[at : at + LINES, 0 : tags.shape[1]] = tags.astype(BF)


def segment_line(f, part):
    base = f * COLS + part * (COLS // 2)
    return (lax.broadcasted_iota(jnp.int32, (COLS // 2, 1), 0) + base).astype(F32)


def stack_into(out_ref, given, part):
    labels = []
    for ref in given:
        count = ref.shape[0] - LINES
        labels.append(tag_of(ref[count : count + LINES, 0:count]))
    share = COLS // 2
    for f in range(FINE):
        line = segment_line(f, part)
        out_ref[f * share : (f + 1) * share, :] = sum(
            jnp.dot(one_hot(label == line), ref[0 : label.shape[1], :], preferred_element_type=F32)
            for label, ref in zip(labels, given)
        ).astype(out_ref.dtype)


def stack_sent_kernel(q, *refs):
    *given, sent_ref, tags_ref = refs
    tags = [tag_of(ref[q.first : q.first + LINES, q.first : q.first + q.second]) for ref in given[:2]]
    tags_ref[...] = jnp.broadcast_to(jnp.concatenate(tags, axis=1), tags_ref.shape)
    stack_into(sent_ref, given, 1 - lax.axis_index("off"))


def stack_kept_kernel(*refs):
    *given, kept_ref = refs
    stack_into(kept_ref, given, lax.axis_index("off"))


def join_kernel(*refs):
    *given, out_ref = refs
    at = 0
    for ref in given:
        out_ref[at : at + ref.shape[0], :] = ref[...]
        at += ref.shape[0]


def stack_second_kernel(q, tags_ref, kept_ref, own_ref, other_ref, out_ref, rows_ref):
    x = lax.axis_index("off")
    rows_ref[: q.second, :] = own_ref[...]
    rows_ref[q.second :, :] = other_ref[...]
    label = tags_ref[0:1, :]
    share = COLS // 2
    for f in range(FINE):
        span = slice(f * share, (f + 1) * share)
        more = jnp.dot(one_hot(label == segment_line(f, x)), rows_ref[...], preferred_element_type=F32)
        out_ref[span, :] = (kept_ref[span, :] + more).astype(BF)


def short_path(cap, records, mid_bin, live_count, fine_class, ops, index):
    q = Slots(cap)
    samples = records.shape[1]
    share, depth = COLS // 2, ops.shape[1] * ops.shape[-1]
    packed, lines, own, flag, held = pl.pallas_call(
        functools.partial(pack_spare_kernel, q),
        out_shape=[
            shape(q.spare, samples),
            shape(LINES, TILE),
            shape(q.cap + LINES, samples),
            shape(8, 128, F32),
            shape(*records.shape),
        ],
        in_specs=[smem()] + [pl.BlockSpec(memory_space=pltpu.HBM)] * 3,
        out_specs=[vmem()] * 5,
        scratch_shapes=[
            pltpu.VMEM(mid_bin.shape, jnp.int32),
            pltpu.VMEM(fine_class.shape, jnp.int32),
            pltpu.SemaphoreType.DMA((10,)),
        ],
        compiler_params=params(24),
        name="pack_spare",
    )(live_count, mid_bin, fine_class, records)
    spare, lines, own_other = swap(packed, "bin", 2), swap(lines, "bin", 2), swap(own, "sub", 1)
    cross2, cross3, near, back2, back3, near_back = call(
        functools.partial(pack_rest_kernel, q),
        [shape(q.front, samples)] * 2
        + [shape(q.near_front + LINES, samples)]
        + [shape(q.back, samples)] * 2
        + [shape(q.near_back, samples)],
        [live_count, mid_bin, fine_class, held],
        1,
        "pack_rest",
        flops=2 * (2 * q.each + q.cap) * records.size,
        after=[packed],
    )
    cross2, cross3, near = swap(cross2, "bin", 2), swap(cross3, "bin", 3), swap(near, "bin", 1)
    for axis in ("sub", "off", "grp"):
        mask = 1
        while mask < lax.axis_size(axis):
            flag = jnp.maximum(flag, swap(flag, axis, mask))
            mask *= 2
    (relay,) = call(
        functools.partial(relay_kernel, q), [shape(q.spare + LINES, samples)], [spare, lines, flag], 0, "relay"
    )
    relay = swap(relay, "bin", 1)
    back2, back3, near_back = gate([back2, back3, near_back], [cross3])
    rows, flag = call(
        functools.partial(gather_kernel, q),
        [shape(q.first + LINES, samples), shape(8, 128, F32)],
        [spare, lines, cross2, cross3, near, relay, flag],
        0,
        "gather",
        after=[back2, own_other],
    )
    flag = jnp.maximum(flag, swap(flag, "bin", 2))
    back2, back3, near_back = swap(back2, "bin", 2), swap(back3, "bin", 3), swap(near_back, "bin", 1)
    given = [rows, swap(rows, "sub", 1), own, own_other]
    flops = 2 * FINE * COLS * (q.first + q.cap) * samples
    sent, tags = call(
        functools.partial(stack_sent_kernel, q),
        [shape(FINE * share, samples), shape(8, 2 * q.second, F32)],
        given,
        0,
        "stack_sent",
        flops=flops,
        after=[flag],
    )
    terms = call(
        send_kernel,
        [shape(share, depth // 2)] * 2,
        [index, ops, sent],
        1,
        "operate",
        flops=2 * share * ops.size,
    )
    came = [swap(piece, "off", 1) for piece in terms]
    (kept,) = call(
        stack_kept_kernel,
        [shape(FINE * share, samples, F32)],
        given,
        0,
        "stack_kept",
        flops=flops,
        after=[terms[0]],
    )
    (late,) = call(
        join_kernel,
        [shape(q.second, samples)],
        [back2, back3, near_back],
        0,
        "join",
        after=[kept, *came],
    )
    (stacked,) = call(
        functools.partial(stack_second_kernel, q),
        [shape(FINE * share, samples)],
        [tags, kept, late, swap(late, "sub", 1)],
        0,
        "stack_second",
        scratch=[pltpu.VMEM((2 * q.second, samples), BF)],
        flops=2 * FINE * COLS * q.second * samples,
    )
    (image,) = call(
        finish_kernel,
        [shape(share, depth, F32)],
        [index, ops, stacked, *came],
        1,
        "finish",
        flops=2 * share * ops.size,
    )
    given = (records, mid_bin, live_count, fine_class, ops, index)
    return lax.cond(flag[0, 0] > 0.0, lambda image, *a: static_path(cap, *a), lambda image, *a: image, image, *given)


def local(traces, mid_bin, live_count, fine_class, operator, block_index):
    records = traces[0]
    owners, offs = lax.axis_size("bin"), lax.axis_size("off")
    cap = 3 * records.shape[0] // (2 * owners)
    path = short_path if owners == 4 and offs == 2 else static_path
    return path(cap, records, mid_bin, live_count, fine_class, operator[0, :, 0], block_index[0, :, 0])


def solution(mesh):
    placed = (
        P(("grp", "off"), ("bin", "sub"), None),
        P(("grp", "off"), ("bin", "sub")),
        P(("grp", "off"), ("bin", "sub")),
        P(("grp", "off"), ("bin", "sub")),
        P(("grp", "off"), None, "bin", "sub", None, None, None),
        P(("grp", "off"), None, "bin", "sub", None),
    )
    return jax.shard_map(
        local,
        mesh=mesh,
        in_specs=placed,
        out_specs=P(("grp", "bin", "off"), "sub"),
        check_vma=False,
    )
```

```python
import functools

import jax
import jax.numpy as jnp
from jax import lax
from jax.experimental import pallas as pl
from jax.experimental.pallas import tpu as pltpu
from jax.sharding import PartitionSpec as P

FINE = 2
COLS = 512
LINES = 16
TILE = 256
BF = jnp.bfloat16
F32 = jnp.float32
MIB = 1 << 20


def params(mib):
    return pltpu.CompilerParams(vmem_limit_bytes=mib * MIB)


def vmem():
    return pl.BlockSpec(memory_space=pltpu.VMEM)


def smem():
    return pl.BlockSpec(memory_space=pltpu.SMEM)


def call(body, out_shape, operands, scalars, name, mib=24, scratch=(), flops=0, after=()):
    moved = sum(a.size * a.dtype.itemsize for a in (*operands, *out_shape))
    count, late = len(operands), len(after)

    def run(*refs):
        body(*refs[:count], *refs[count + late :])

    return pl.pallas_call(
        run,
        out_shape=list(out_shape),
        in_specs=[smem()] * scalars + [vmem()] * (count - scalars + late),
        out_specs=[vmem()] * len(out_shape),
        scratch_shapes=list(scratch),
        compiler_params=params(mib),
        cost_estimate=pl.CostEstimate(flops=flops, bytes_accessed=moved, transcendentals=0),
        name=name,
    )(*operands, *(corner(a) for a in after))


def corner(a):
    return a[:LINES, :128]


def gate(given, after):
    return pl.pallas_call(
        lambda *refs: None,
        out_shape=[jax.ShapeDtypeStruct(a.shape, a.dtype) for a in given],
        in_specs=[vmem()] * (len(given) + len(after)),
        out_specs=[vmem()] * len(given),
        input_output_aliases={i: i for i in range(len(given))},
        compiler_params=params(4),
        cost_estimate=pl.CostEstimate(flops=0, bytes_accessed=0, transcendentals=0),
        name="gate",
    )(*given, *(corner(a) for a in after))


def shape(rows, columns, kind=BF):
    return jax.ShapeDtypeStruct((rows, columns), kind)


def one_hot(mask):
    return jnp.where(mask, 1.0, 0.0).astype(BF)


def running_count(mask_rows):
    rows = mask_rows.shape[1]
    upper = lax.broadcasted_iota(jnp.int32, (rows, rows), 0) <= lax.broadcasted_iota(jnp.int32, (rows, rows), 1)
    return jnp.dot(one_hot(mask_rows), one_hot(upper), preferred_element_type=F32)


def choose(position, slots):
    place = lax.broadcasted_iota(jnp.int32, (slots, position.shape[1]), 0).astype(F32)
    return one_hot(position == place)


def tag_digits(live, owner, mid, fine, lines=LINES):
    tag = jnp.where(live, fine * COLS + mid - owner * COLS + 1, 0)
    line = lax.broadcasted_iota(jnp.int32, (lines, tag.shape[1]), 0)
    return jnp.where(line == 0, tag // 256, jnp.where(line == 1, tag % 256, 0)).astype(F32).astype(BF)


def across(digits, chosen):
    return lax.dot_general(digits, chosen, (((1,), (1,)), ((), ())), preferred_element_type=F32)


def tag_of(lines):
    lines = lines.astype(F32)
    return 256.0 * lines[0:1] + lines[1:2] - 1.0


def full_pack_kernel(owners, cap, live_ref, mid_ref, fine_ref, traces_ref, *outs):
    z = lax.axis_index("bin")
    rows, samples = traces_ref.shape
    live = lax.broadcasted_iota(jnp.int32, (1, rows), 1) < live_ref[0, 0]
    mid = mid_ref[...]
    owner = mid // COLS
    target = lax.broadcasted_iota(jnp.int32, (max(owners, 16), rows), 0) ^ z
    hits = jnp.where(live, owner, -1) == target
    slot = jnp.where(hits, running_count(hits) - 1.0, -1.0)
    digits = tag_digits(live, owner, mid, fine_ref[...])
    for d in range(owners):
        select = choose(slot[d : d + 1], cap)
        outs[d][0:cap, :] = jnp.dot(select, traces_ref[...], preferred_element_type=F32).astype(BF)
        outs[d][cap : cap + LINES, :] = jnp.zeros((LINES, samples), BF)
        outs[d][cap : cap + LINES, 0:cap] = across(digits, select).astype(BF)


def full_stack_kernel(cap, *refs):
    *given, stacked_ref, rows_ref = refs
    label = jnp.concatenate([tag_of(ref[cap : cap + LINES, 0:cap]) for ref in given], axis=1)
    for i, ref in enumerate(given):
        rows_ref[i * cap : (i + 1) * cap, :] = ref[0:cap, :]

    def tile(t, carry):
        base = pl.multiple_of(t * TILE, TILE)
        line = (lax.broadcasted_iota(jnp.int32, (TILE, 1), 0) + base).astype(F32)
        stacked_ref[pl.ds(base, TILE), :] = jnp.dot(
            one_hot(label == line), rows_ref[...], preferred_element_type=F32
        ).astype(BF)
        return carry

    lax.fori_loop(0, FINE * COLS // TILE, tile, 0)


def image_terms(d, index_ref, ops_ref, stacked_ref):
    fine, _, taps = index_ref.shape
    width = ops_ref.shape[-1]
    columns = stacked_ref.shape[0] // fine
    picked, weights = [], []
    for f in range(fine):
        for k in range(taps):
            at = pl.multiple_of(index_ref[f, d, k] * width, width)
            picked.append(stacked_ref[f * columns : (f + 1) * columns, pl.ds(at, width)])
            weights.append(ops_ref[f, d, k])
    return lax.dot_general(
        jnp.concatenate(picked, axis=1),
        jnp.concatenate(weights, axis=1),
        (((1,), (1,)), ((), ())),
        preferred_element_type=F32,
    )


def operate_kernel(index_ref, ops_ref, stacked_ref, out_ref):
    width = ops_ref.shape[-1]
    for d in range(index_ref.shape[1]):
        terms = image_terms(d, index_ref, ops_ref, stacked_ref)
        out_ref[0 : terms.shape[0], d * width : (d + 1) * width] = terms.astype(out_ref.dtype)


def operate(index, ops, stacked, kind):
    columns, depth = stacked.shape[0] // FINE, ops.shape[1] * ops.shape[-1]
    (out,) = call(
        operate_kernel,
        [shape(columns, depth, kind)],
        [index, ops, stacked],
        1,
        "operate",
        flops=2 * columns * ops.size,
    )
    return out


def send_kernel(index_ref, ops_ref, stacked_ref, *outs):
    width = ops_ref.shape[-1]
    each = outs[0].shape[1]
    for d in range(index_ref.shape[1]):
        piece, at = outs[d * width // each], d * width % each
        piece[:, at : at + width] = image_terms(d, index_ref, ops_ref, stacked_ref).astype(BF)


def finish_kernel(index_ref, ops_ref, stacked_ref, *refs):
    *came, out_ref = refs
    width = ops_ref.shape[-1]
    each = came[0].shape[1]
    for d in range(index_ref.shape[1]):
        piece, at = came[d * width // each], d * width % each
        more = piece[:, at : at + width].astype(F32)
        out_ref[:, d * width : (d + 1) * width] = image_terms(d, index_ref, ops_ref, stacked_ref) + more


def swap(x, axis, mask):
    return lax.ppermute(x, axis, [(i, i ^ mask) for i in range(lax.axis_size(axis))])


def static_path(cap, records, mid_bin, live_count, fine_class, ops, index):
    owners, subs, offs = (lax.axis_size(a) for a in ("bin", "sub", "off"))
    samples = records.shape[1]
    packed = call(
        functools.partial(full_pack_kernel, owners, cap),
        [shape(cap + LINES, samples)] * owners,
        [live_count, mid_bin, fine_class, records],
        1,
        "full_pack",
    )
    arrived = [packed[0]] + [swap(packed[d], "bin", d) for d in range(1, owners)]
    arrived += [swap(a, "sub", e) for e in range(1, subs) for a in arrived]
    (stacked,) = call(
        functools.partial(full_stack_kernel, cap),
        [shape(FINE * COLS, samples)],
        arrived,
        0,
        "full_stack",
        mib=32,
        scratch=[pltpu.VMEM((cap * len(arrived), samples), BF)],
    )
    terms = operate(index, ops, stacked, F32)
    share = COLS // offs
    x = lax.axis_index("off")
    total = lax.dynamic_slice_in_dim(terms, x * share, share, axis=0)
    for k in range(1, offs):
        total = total + swap(lax.dynamic_slice_in_dim(terms, (x ^ k) * share, share, axis=0), "off", k)
    return total


class Slots:
    def __init__(self, cap):
        self.cap = cap
        self.each = 2 * cap // 3
        self.spare = cap - self.each
        self.front = 5 * cap // 12
        self.back = self.each - self.front
        self.near_front = 2 * cap // 3
        self.near_back = cap - self.near_front
        self.first = 2 * self.spare + 2 * self.front + self.near_front
        self.second = 2 * self.back + self.near_back


def positions(q, live_ref, mid_ref):
    rows = mid_ref.shape[1]
    z, x = lax.axis_index("bin"), lax.axis_index("off")
    live = lax.broadcasted_iota(jnp.int32, (1, rows), 1) < live_ref[0, 0]
    mid = mid_ref[...]
    owner = mid // COLS
    share = COLS // 2
    kept = jnp.where((mid - owner * COLS) // share == x, 1, 0)
    kind = jnp.where(live, (owner ^ z) * 2 + kept, -1)
    hits = lax.broadcasted_iota(jnp.int32, (16, rows), 0) == kind
    rank = running_count(hits)
    seat = jnp.where(hits, rank - 1.0, -1.0)
    place, late, spare = [], [], -1.0
    base = jnp.zeros((1, 1), F32)
    for d in range(4):
        first, second = seat[2 * d : 2 * d + 1], seat[2 * d + 1 : 2 * d + 2]
        if d < 2:
            place.append(jnp.where(first >= 0, first, jnp.where(second >= 0, q.cap - 1.0 - second, -1.0)))
            continue
        ahead = rank[2 * d : 2 * d + 1, rows - 1 : rows]
        behind = rank[2 * d + 1 : 2 * d + 2, rows - 1 : rows]
        room = q.each - jnp.minimum(ahead, float(q.front))
        late_first, late_second = first >= q.front, second >= room
        place.append(
            jnp.where(
                late_first | late_second, -1.0, jnp.where(first >= 0, first, jnp.where(second >= 0, q.each - 1.0 - second, -1.0))
            )
        )
        late.append(late_first | late_second)
        over = jnp.maximum(ahead - q.front, 0.0)
        spare = jnp.where(
            late_first, base + first - q.front, jnp.where(late_second, base + over + second - room, spare)
        )
        base = base + over + jnp.maximum(behind - room, 0.0)
    excess = jnp.maximum(base - q.spare, rank[2:3, rows - 1 : rows] - q.near_front)
    return live, mid, owner, place, spare, late, excess


def lay(ref, rows, tags):
    size = rows.shape[0]
    ref[0:size, :] = rows
    ref[size : size + LINES, :] = jnp.zeros((LINES, ref.shape[1]), BF)
    ref[size : size + LINES, 0 : tags.shape[1]] = tags.astype(BF)


def pack_spare_kernel(
    q, live_ref, mid_hbm, fine_hbm, traces_ref, spare_ref, lines_ref, own_ref, flag_ref, held_ref, mid_ref, fine_ref, sems
):
    copies = [
        pltpu.make_async_copy(mid_hbm, mid_ref, sems.at[0]),
        pltpu.make_async_copy(fine_hbm, fine_ref, sems.at[1]),
    ]
    count = sems.shape[0] - 2
    step = held_ref.shape[0] // count
    for i in range(count):
        span = pl.ds(i * step, step)
        copies.append(pltpu.make_async_copy(traces_ref.at[span], held_ref.at[span], sems.at[i + 2]))
    for copy in copies:
        copy.start()
    for copy in copies[:2]:
        copy.wait()
    live, mid, owner, place, spare, late, excess = positions(q, live_ref, mid_ref)
    digits = tag_digits(live, owner, mid, fine_ref[...])
    extra = [choose(jnp.where(late[i], spare, -1.0), q.spare) for i in range(2)]
    tags = [across(digits, jnp.concatenate([choose(place[d], q.each), extra[d - 2]], axis=0)) for d in (2, 3)]
    crossing = jnp.concatenate([tags[0][0:4], tags[1][0:4], jnp.zeros((LINES - 8, q.cap), F32)], axis=0)
    own = choose(place[0], q.cap)
    chosen = jnp.concatenate([extra[0] + extra[1], own], axis=0)
    lines_ref[...] = jnp.zeros(lines_ref.shape, BF)
    lines_ref[:, 0 : q.cap] = crossing.astype(BF)
    for copy in copies[2:]:
        copy.wait()
    rows = jnp.dot(chosen, held_ref[...], preferred_element_type=F32).astype(BF)
    spare_ref[...] = rows[: q.spare]
    lay(own_ref, rows[q.spare :], across(digits, own))
    flag_ref[...] = jnp.broadcast_to(jnp.where(excess > 0.0, 1.0, 0.0), flag_ref.shape)


def pack_rest_kernel(
    q, live_ref, mid_ref, fine_ref, traces_ref, cross2_ref, cross3_ref, near_ref, back2_ref, back3_ref, near_back_ref
):
    live, mid, owner, place, _, _, _ = positions(q, live_ref, mid_ref)
    digits = tag_digits(live, owner, mid, fine_ref[...])
    near = choose(place[1], q.cap)
    chosen = jnp.concatenate([choose(place[2], q.each), choose(place[3], q.each), near], axis=0)
    rows = jnp.dot(chosen, traces_ref[...], preferred_element_type=F32).astype(BF)
    cross2_ref[...] = rows[: q.front]
    back2_ref[...] = rows[q.front : q.each]
    cross3_ref[...] = rows[q.each : q.each + q.front]
    back3_ref[...] = rows[q.each + q.front : 2 * q.each]
    at = 2 * q.each + q.near_front
    lay(near_ref, rows[2 * q.each : at], across(digits, near))
    near_back_ref[...] = rows[at:]


def relay_kernel(q, spare_ref, lines_ref, flag_ref, out_ref):
    out_ref[0 : q.spare, :] = spare_ref[...]
    row = lax.broadcasted_iota(jnp.int32, lines_ref.shape, 0)
    out_ref[q.spare : q.spare + LINES, :] = jnp.zeros((LINES, out_ref.shape[1]), BF)
    out_ref[q.spare : q.spare + LINES, 0 : lines_ref.shape[1]] = jnp.where(
        row == 3, flag_ref[0:1, 0:1].astype(BF), lines_ref[...]
    )


def gather_kernel(
    q, spare_ref, lines_ref, cross2_ref, cross3_ref, near_ref, relay_ref, own_flag_ref, rows_ref, flag_ref
):
    at = 0
    for ref, size in (
        (spare_ref, q.spare),
        (cross2_ref, q.front),
        (cross3_ref, q.front),
        (near_ref, q.near_front),
        (relay_ref, q.spare),
    ):
        rows_ref[at : at + size, :] = ref[0:size, :]
        at += size
    cross2, cross3, near = (
        ref[size : size + LINES, 0 : q.cap].astype(F32)
        for ref, size in ((lines_ref, 0), (relay_ref, q.spare), (near_ref, q.near_front))
    )
    flag_ref[...] = jnp.maximum(own_flag_ref[...], jnp.broadcast_to(cross3[3:4, 0:128], flag_ref.shape))
    cross2, cross3, near = cross2[0:2], cross3[4:6], near[0:2]
    tags = jnp.concatenate(
        [
            cross2[:, q.each :],
            cross2[:, : q.front],
            cross3[:, : q.front],
            near[:, : q.near_front],
            cross3[:, q.each :],
            cross2[:, q.front : q.each],
            cross3[:, q.front : q.each],
            near[:, q.near_front :],
        ],
        axis=1,
    )
    tags = jnp.concatenate([tags, jnp.zeros((LINES - 2, tags.shape[1]), F32)], axis=0)
    rows_ref[at : at + LINES, :] = jnp.zeros((LINES, rows_ref.shape[1]), BF)
    rows_ref[at : at + LINES, 0 : tags.shape[1]] = tags.astype(BF)


def segment_line(f, part):
    base = f * COLS + part * (COLS // 2)
    return (lax.broadcasted_iota(jnp.int32, (COLS // 2, 1), 0) + base).astype(F32)


def stack_into(out_ref, label, rows_ref, part):
    share = COLS // 2
    for f in range(FINE):
        chosen = one_hot(label == segment_line(f, part))
        out_ref[f * share : (f + 1) * share, :] = jnp.dot(
            chosen, rows_ref[...], preferred_element_type=F32
        ).astype(out_ref.dtype)


def stack_sent_kernel(q, *refs):
    *given, sent_ref, all_ref, labels_ref, tags_ref = refs
    labels, later, at = [], [], 0
    for ref, size in zip(given, (q.first, q.first, q.cap, q.cap)):
        labels.append(tag_of(ref[size : size + LINES, 0:size]))
        all_ref[at : at + size, :] = ref[0:size, :]
        at += size
    for ref in given[:2]:
        later.append(tag_of(ref[q.first : q.first + LINES, q.first : q.first + q.second]))
    label = jnp.concatenate(labels, axis=1)
    labels_ref[...] = jnp.broadcast_to(label, labels_ref.shape)
    tags_ref[...] = jnp.broadcast_to(jnp.concatenate(later, axis=1), tags_ref.shape)
    stack_into(sent_ref, label, all_ref, 1 - lax.axis_index("off"))


def stack_kept_kernel(all_ref, labels_ref, kept_ref):
    stack_into(kept_ref, labels_ref[0:1, :], all_ref, lax.axis_index("off"))


def join_kernel(*refs):
    *given, out_ref = refs
    at = 0
    for ref in given:
        out_ref[at : at + ref.shape[0], :] = ref[...]
        at += ref.shape[0]


def stack_second_kernel(q, tags_ref, kept_ref, own_ref, other_ref, out_ref, rows_ref):
    x = lax.axis_index("off")
    rows_ref[: q.second, :] = own_ref[...]
    rows_ref[q.second :, :] = other_ref[...]
    label = tags_ref[0:1, :]
    share = COLS // 2
    for f in range(FINE):
        span = slice(f * share, (f + 1) * share)
        more = jnp.dot(one_hot(label == segment_line(f, x)), rows_ref[...], preferred_element_type=F32)
        out_ref[span, :] = (kept_ref[span, :] + more).astype(BF)


def short_path(cap, records, mid_bin, live_count, fine_class, ops, index):
    q = Slots(cap)
    samples = records.shape[1]
    share, depth = COLS // 2, ops.shape[1] * ops.shape[-1]
    packed, lines, own, flag, held = pl.pallas_call(
        functools.partial(pack_spare_kernel, q),
        out_shape=[
            shape(q.spare, samples),
            shape(LINES, TILE),
            shape(q.cap + LINES, samples),
            shape(8, 128, F32),
            shape(*records.shape),
        ],
        in_specs=[smem()] + [pl.BlockSpec(memory_space=pltpu.HBM)] * 3,
        out_specs=[vmem()] * 5,
        scratch_shapes=[
            pltpu.VMEM(mid_bin.shape, jnp.int32),
            pltpu.VMEM(fine_class.shape, jnp.int32),
            pltpu.SemaphoreType.DMA((10,)),
        ],
        compiler_params=params(24),
        name="pack_spare",
    )(live_count, mid_bin, fine_class, records)
    spare, lines, own_other = swap(packed, "bin", 2), swap(lines, "bin", 2), swap(own, "sub", 1)
    cross2, cross3, near, back2, back3, near_back = call(
        functools.partial(pack_rest_kernel, q),
        [shape(q.front, samples)] * 2
        + [shape(q.near_front + LINES, samples)]
        + [shape(q.back, samples)] * 2
        + [shape(q.near_back, samples)],
        [live_count, mid_bin, fine_class, held],
        1,
        "pack_rest",
        flops=2 * (2 * q.each + q.cap) * records.size,
        after=[packed],
    )
    cross2, cross3, near = swap(cross2, "bin", 2), swap(cross3, "bin", 3), swap(near, "bin", 1)
    for axis in ("sub", "off", "grp"):
        mask = 1
        while mask < lax.axis_size(axis):
            flag = jnp.maximum(flag, swap(flag, axis, mask))
            mask *= 2
    (relay,) = call(
        functools.partial(relay_kernel, q), [shape(q.spare + LINES, samples)], [spare, lines, flag], 0, "relay"
    )
    relay = swap(relay, "bin", 1)
    back2, back3, near_back = gate([back2, back3, near_back], [cross3])
    rows, flag = call(
        functools.partial(gather_kernel, q),
        [shape(q.first + LINES, samples), shape(8, 128, F32)],
        [spare, lines, cross2, cross3, near, relay, flag],
        0,
        "gather",
        after=[back2, own_other],
    )
    flag = jnp.maximum(flag, swap(flag, "bin", 2))
    back2, back3, near_back = swap(back2, "bin", 2), swap(back3, "bin", 3), swap(near_back, "bin", 1)
    given = [rows, swap(rows, "sub", 1), own, own_other]
    slots = 2 * (q.first + q.cap)
    flops = FINE * COLS * slots * samples
    sent, every, labels, tags = call(
        functools.partial(stack_sent_kernel, q),
        [
            shape(FINE * share, samples),
            shape(slots, samples),
            shape(8, slots, F32),
            shape(8, 2 * q.second, F32),
        ],
        given,
        0,
        "stack_sent",
        flops=flops,
        after=[flag],
    )
    terms = call(
        send_kernel,
        [shape(share, depth // 2)] * 2,
        [index, ops, sent],
        1,
        "operate",
        flops=2 * share * ops.size,
    )
    came = [swap(piece, "off", 1) for piece in terms]
    (kept,) = call(
        stack_kept_kernel,
        [shape(FINE * share, samples, F32)],
        [every, labels],
        0,
        "stack_kept",
        flops=flops,
        after=[terms[0]],
    )
    (late,) = call(
        join_kernel,
        [shape(q.second, samples)],
        [back2, back3, near_back],
        0,
        "join",
        after=[kept, *came],
    )
    (stacked,) = call(
        functools.partial(stack_second_kernel, q),
        [shape(FINE * share, samples)],
        [tags, kept, late, swap(late, "sub", 1)],
        0,
        "stack_second",
        scratch=[pltpu.VMEM((2 * q.second, samples), BF)],
        flops=2 * FINE * COLS * q.second * samples,
    )
    (image,) = call(
        finish_kernel,
        [shape(share, depth, F32)],
        [index, ops, stacked, *came],
        1,
        "finish",
        flops=2 * share * ops.size,
    )
    given = (records, mid_bin, live_count, fine_class, ops, index)
    return lax.cond(flag[0, 0] > 0.0, lambda image, *a: static_path(cap, *a), lambda image, *a: image, image, *given)


def local(traces, mid_bin, live_count, fine_class, operator, block_index):
    records = traces[0]
    owners, offs = lax.axis_size("bin"), lax.axis_size("off")
    cap = 3 * records.shape[0] // (2 * owners)
    path = short_path if owners == 4 and offs == 2 else static_path
    return path(cap, records, mid_bin, live_count, fine_class, operator[0, :, 0], block_index[0, :, 0])


def solution(mesh):
    placed = (
        P(("grp", "off"), ("bin", "sub"), None),
        P(("grp", "off"), ("bin", "sub")),
        P(("grp", "off"), ("bin", "sub")),
        P(("grp", "off"), ("bin", "sub")),
        P(("grp", "off"), None, "bin", "sub", None, None, None),
        P(("grp", "off"), None, "bin", "sub", None),
    )
    return jax.shard_map(
        local,
        mesh=mesh,
        in_specs=placed,
        out_specs=P(("grp", "bin", "off"), "sub"),
        check_vma=False,
    )
```

```python
import functools

import jax
import jax.numpy as jnp
from jax import lax
from jax.experimental import pallas as pl
from jax.experimental.pallas import tpu as pltpu
from jax.sharding import PartitionSpec as P

FINE = 2
COLS = 512
LINES = 16
TILE = 256
BF = jnp.bfloat16
F32 = jnp.float32
MIB = 1 << 20


def params(mib):
    return pltpu.CompilerParams(vmem_limit_bytes=mib * MIB)


def vmem():
    return pl.BlockSpec(memory_space=pltpu.VMEM)


def smem():
    return pl.BlockSpec(memory_space=pltpu.SMEM)


def call(body, out_shape, operands, scalars, name, mib=24, scratch=(), flops=0, after=()):
    moved = sum(a.size * a.dtype.itemsize for a in (*operands, *out_shape))
    count, late = len(operands), len(after)

    def run(*refs):
        body(*refs[:count], *refs[count + late :])

    return pl.pallas_call(
        run,
        out_shape=list(out_shape),
        in_specs=[smem()] * scalars + [vmem()] * (count - scalars + late),
        out_specs=[vmem()] * len(out_shape),
        scratch_shapes=list(scratch),
        compiler_params=params(mib),
        cost_estimate=pl.CostEstimate(flops=flops, bytes_accessed=moved, transcendentals=0),
        name=name,
    )(*operands, *(corner(a) for a in after))


def corner(a):
    return a[:LINES, :128]


def gate(given, after):
    return pl.pallas_call(
        lambda *refs: None,
        out_shape=[jax.ShapeDtypeStruct(a.shape, a.dtype) for a in given],
        in_specs=[vmem()] * (len(given) + len(after)),
        out_specs=[vmem()] * len(given),
        input_output_aliases={i: i for i in range(len(given))},
        compiler_params=params(4),
        cost_estimate=pl.CostEstimate(flops=0, bytes_accessed=0, transcendentals=0),
        name="gate",
    )(*given, *(corner(a) for a in after))


def shape(rows, columns, kind=BF):
    return jax.ShapeDtypeStruct((rows, columns), kind)


def one_hot(mask):
    return jnp.where(mask, 1.0, 0.0).astype(BF)


def running_count(mask_rows):
    rows = mask_rows.shape[1]
    upper = lax.broadcasted_iota(jnp.int32, (rows, rows), 0) <= lax.broadcasted_iota(jnp.int32, (rows, rows), 1)
    return jnp.dot(one_hot(mask_rows), one_hot(upper), preferred_element_type=F32)


def choose(position, slots):
    place = lax.broadcasted_iota(jnp.int32, (slots, position.shape[1]), 0).astype(F32)
    return one_hot(position == place)


def tag_digits(live, owner, mid, fine, lines=LINES):
    tag = jnp.where(live, fine * COLS + mid - owner * COLS + 1, 0)
    line = lax.broadcasted_iota(jnp.int32, (lines, tag.shape[1]), 0)
    return jnp.where(line == 0, tag // 256, jnp.where(line == 1, tag % 256, 0)).astype(F32).astype(BF)


def across(digits, chosen):
    return lax.dot_general(digits, chosen, (((1,), (1,)), ((), ())), preferred_element_type=F32)


def tag_of(lines):
    lines = lines.astype(F32)
    return 256.0 * lines[0:1] + lines[1:2] - 1.0


def full_pack_kernel(owners, cap, live_ref, mid_ref, fine_ref, traces_ref, *outs):
    z = lax.axis_index("bin")
    rows, samples = traces_ref.shape
    live = lax.broadcasted_iota(jnp.int32, (1, rows), 1) < live_ref[0, 0]
    mid = mid_ref[...]
    owner = mid // COLS
    target = lax.broadcasted_iota(jnp.int32, (max(owners, 16), rows), 0) ^ z
    hits = jnp.where(live, owner, -1) == target
    slot = jnp.where(hits, running_count(hits) - 1.0, -1.0)
    digits = tag_digits(live, owner, mid, fine_ref[...])
    for d in range(owners):
        select = choose(slot[d : d + 1], cap)
        outs[d][0:cap, :] = jnp.dot(select, traces_ref[...], preferred_element_type=F32).astype(BF)
        outs[d][cap : cap + LINES, :] = jnp.zeros((LINES, samples), BF)
        outs[d][cap : cap + LINES, 0:cap] = across(digits, select).astype(BF)


def full_stack_kernel(cap, *refs):
    *given, stacked_ref, rows_ref = refs
    label = jnp.concatenate([tag_of(ref[cap : cap + LINES, 0:cap]) for ref in given], axis=1)
    for i, ref in enumerate(given):
        rows_ref[i * cap : (i + 1) * cap, :] = ref[0:cap, :]

    def tile(t, carry):
        base = pl.multiple_of(t * TILE, TILE)
        line = (lax.broadcasted_iota(jnp.int32, (TILE, 1), 0) + base).astype(F32)
        stacked_ref[pl.ds(base, TILE), :] = jnp.dot(
            one_hot(label == line), rows_ref[...], preferred_element_type=F32
        ).astype(BF)
        return carry

    lax.fori_loop(0, FINE * COLS // TILE, tile, 0)


def image_terms(d, index_ref, ops_ref, stacked_ref):
    fine, _, taps = index_ref.shape
    width = ops_ref.shape[-1]
    columns = stacked_ref.shape[0] // fine
    picked, weights = [], []
    for f in range(fine):
        for k in range(taps):
            at = pl.multiple_of(index_ref[f, d, k] * width, width)
            picked.append(stacked_ref[f * columns : (f + 1) * columns, pl.ds(at, width)])
            weights.append(ops_ref[f, d, k])
    return lax.dot_general(
        jnp.concatenate(picked, axis=1),
        jnp.concatenate(weights, axis=1),
        (((1,), (1,)), ((), ())),
        preferred_element_type=F32,
    )


def operate_kernel(index_ref, ops_ref, stacked_ref, out_ref):
    width = ops_ref.shape[-1]
    for d in range(index_ref.shape[1]):
        terms = image_terms(d, index_ref, ops_ref, stacked_ref)
        out_ref[0 : terms.shape[0], d * width : (d + 1) * width] = terms.astype(out_ref.dtype)


def operate(index, ops, stacked, kind):
    columns, depth = stacked.shape[0] // FINE, ops.shape[1] * ops.shape[-1]
    (out,) = call(
        operate_kernel,
        [shape(columns, depth, kind)],
        [index, ops, stacked],
        1,
        "operate",
        flops=2 * columns * ops.size,
    )
    return out


def send_kernel(index_ref, ops_ref, stacked_ref, *outs):
    width = ops_ref.shape[-1]
    each = outs[0].shape[1]
    for d in range(index_ref.shape[1]):
        piece, at = outs[d * width // each], d * width % each
        piece[:, at : at + width] = image_terms(d, index_ref, ops_ref, stacked_ref).astype(BF)


def finish_kernel(index_ref, ops_ref, stacked_ref, *refs):
    *came, out_ref = refs
    width = ops_ref.shape[-1]
    each = came[0].shape[1]
    for d in range(index_ref.shape[1]):
        piece, at = came[d * width // each], d * width % each
        more = piece[:, at : at + width].astype(F32)
        out_ref[:, d * width : (d + 1) * width] = image_terms(d, index_ref, ops_ref, stacked_ref) + more


def swap(x, axis, mask):
    return lax.ppermute(x, axis, [(i, i ^ mask) for i in range(lax.axis_size(axis))])


def static_path(cap, records, mid_bin, live_count, fine_class, ops, index):
    owners, subs, offs = (lax.axis_size(a) for a in ("bin", "sub", "off"))
    samples = records.shape[1]
    packed = call(
        functools.partial(full_pack_kernel, owners, cap),
        [shape(cap + LINES, samples)] * owners,
        [live_count, mid_bin, fine_class, records],
        1,
        "full_pack",
    )
    arrived = [packed[0]] + [swap(packed[d], "bin", d) for d in range(1, owners)]
    arrived += [swap(a, "sub", e) for e in range(1, subs) for a in arrived]
    (stacked,) = call(
        functools.partial(full_stack_kernel, cap),
        [shape(FINE * COLS, samples)],
        arrived,
        0,
        "full_stack",
        mib=32,
        scratch=[pltpu.VMEM((cap * len(arrived), samples), BF)],
    )
    terms = operate(index, ops, stacked, F32)
    share = COLS // offs
    x = lax.axis_index("off")
    total = lax.dynamic_slice_in_dim(terms, x * share, share, axis=0)
    for k in range(1, offs):
        total = total + swap(lax.dynamic_slice_in_dim(terms, (x ^ k) * share, share, axis=0), "off", k)
    return total


class Slots:
    def __init__(self, cap):
        self.cap = cap
        self.each = 2 * cap // 3
        self.spare = cap - self.each
        self.front = 5 * cap // 12
        self.back = self.each - self.front
        self.near_front = 2 * cap // 3
        self.near_back = cap - self.near_front
        self.first = 2 * self.spare + 2 * self.front + self.near_front
        self.second = 2 * self.back + self.near_back


def positions(q, live_ref, mid_ref):
    rows = mid_ref.shape[1]
    z, x = lax.axis_index("bin"), lax.axis_index("off")
    live = lax.broadcasted_iota(jnp.int32, (1, rows), 1) < live_ref[0, 0]
    mid = mid_ref[...]
    owner = mid // COLS
    share = COLS // 2
    kept = jnp.where((mid - owner * COLS) // share == x, 1, 0)
    kind = jnp.where(live, (owner ^ z) * 2 + kept, -1)
    hits = lax.broadcasted_iota(jnp.int32, (16, rows), 0) == kind
    rank = running_count(hits)
    seat = jnp.where(hits, rank - 1.0, -1.0)
    place, late, spare = [], [], -1.0
    base = jnp.zeros((1, 1), F32)
    for d in range(4):
        first, second = seat[2 * d : 2 * d + 1], seat[2 * d + 1 : 2 * d + 2]
        if d < 2:
            place.append(jnp.where(first >= 0, first, jnp.where(second >= 0, q.cap - 1.0 - second, -1.0)))
            continue
        ahead = rank[2 * d : 2 * d + 1, rows - 1 : rows]
        behind = rank[2 * d + 1 : 2 * d + 2, rows - 1 : rows]
        room = q.each - jnp.minimum(ahead, float(q.front))
        late_first, late_second = first >= q.front, second >= room
        place.append(
            jnp.where(
                late_first | late_second, -1.0, jnp.where(first >= 0, first, jnp.where(second >= 0, q.each - 1.0 - second, -1.0))
            )
        )
        late.append(late_first | late_second)
        over = jnp.maximum(ahead - q.front, 0.0)
        spare = jnp.where(
            late_first, base + first - q.front, jnp.where(late_second, base + over + second - room, spare)
        )
        base = base + over + jnp.maximum(behind - room, 0.0)
    excess = jnp.maximum(base - q.spare, rank[2:3, rows - 1 : rows] - q.near_front)
    return live, mid, owner, place, spare, late, excess


def lay(ref, rows, tags):
    size = rows.shape[0]
    ref[0:size, :] = rows
    ref[size : size + LINES, :] = jnp.zeros((LINES, ref.shape[1]), BF)
    ref[size : size + LINES, 0 : tags.shape[1]] = tags.astype(BF)


def pack_spare_kernel(
    q, live_ref, mid_hbm, fine_hbm, traces_ref, spare_ref, lines_ref, own_ref, flag_ref, held_ref, mid_ref, fine_ref, sems
):
    copies = [
        pltpu.make_async_copy(mid_hbm, mid_ref, sems.at[0]),
        pltpu.make_async_copy(fine_hbm, fine_ref, sems.at[1]),
    ]
    count = sems.shape[0] - 2
    step = held_ref.shape[0] // count
    for i in range(count):
        span = pl.ds(i * step, step)
        copies.append(pltpu.make_async_copy(traces_ref.at[span], held_ref.at[span], sems.at[i + 2]))
    for copy in copies:
        copy.start()
    for copy in copies[:2]:
        copy.wait()
    live, mid, owner, place, spare, late, excess = positions(q, live_ref, mid_ref)
    digits = tag_digits(live, owner, mid, fine_ref[...])
    extra = [choose(jnp.where(late[i], spare, -1.0), q.spare) for i in range(2)]
    tags = [across(digits, jnp.concatenate([choose(place[d], q.each), extra[d - 2]], axis=0)) for d in (2, 3)]
    crossing = jnp.concatenate([tags[0][0:4], tags[1][0:4], jnp.zeros((LINES - 8, q.cap), F32)], axis=0)
    own = choose(place[0], q.cap)
    chosen = jnp.concatenate([extra[0] + extra[1], own], axis=0)
    lines_ref[...] = jnp.zeros(lines_ref.shape, BF)
    lines_ref[:, 0 : q.cap] = crossing.astype(BF)
    rows = 0.0
    size = held_ref.shape[0] // 2
    for part in range(2):
        for copy in copies[2 + part * count // 2 : 2 + (part + 1) * count // 2]:
            copy.wait()
        span = slice(part * size, (part + 1) * size)
        rows = rows + jnp.dot(chosen[:, span], held_ref[span, :], preferred_element_type=F32)
    rows = rows.astype(BF)
    spare_ref[...] = rows[: q.spare]
    lay(own_ref, rows[q.spare :], across(digits, own))
    flag_ref[...] = jnp.broadcast_to(jnp.where(excess > 0.0, 1.0, 0.0), flag_ref.shape)


def pack_rest_kernel(
    q, live_ref, mid_ref, fine_ref, traces_ref, cross2_ref, cross3_ref, near_ref, back2_ref, back3_ref, near_back_ref
):
    live, mid, owner, place, _, _, _ = positions(q, live_ref, mid_ref)
    digits = tag_digits(live, owner, mid, fine_ref[...])
    near = choose(place[1], q.cap)
    chosen = jnp.concatenate([choose(place[2], q.each), choose(place[3], q.each), near], axis=0)
    rows = jnp.dot(chosen, traces_ref[...], preferred_element_type=F32).astype(BF)
    cross2_ref[...] = rows[: q.front]
    back2_ref[...] = rows[q.front : q.each]
    cross3_ref[...] = rows[q.each : q.each + q.front]
    back3_ref[...] = rows[q.each + q.front : 2 * q.each]
    at = 2 * q.each + q.near_front
    lay(near_ref, rows[2 * q.each : at], across(digits, near))
    near_back_ref[...] = rows[at:]


def relay_kernel(q, spare_ref, lines_ref, flag_ref, out_ref):
    out_ref[0 : q.spare, :] = spare_ref[...]
    row = lax.broadcasted_iota(jnp.int32, lines_ref.shape, 0)
    out_ref[q.spare : q.spare + LINES, :] = jnp.zeros((LINES, out_ref.shape[1]), BF)
    out_ref[q.spare : q.spare + LINES, 0 : lines_ref.shape[1]] = jnp.where(
        row == 3, flag_ref[0:1, 0:1].astype(BF), lines_ref[...]
    )


def gather_kernel(
    q, spare_ref, lines_ref, cross2_ref, cross3_ref, near_ref, relay_ref, own_flag_ref, rows_ref, flag_ref
):
    at = 0
    for ref, size in (
        (spare_ref, q.spare),
        (cross2_ref, q.front),
        (cross3_ref, q.front),
        (near_ref, q.near_front),
        (relay_ref, q.spare),
    ):
        rows_ref[at : at + size, :] = ref[0:size, :]
        at += size
    cross2, cross3, near = (
        ref[size : size + LINES, 0 : q.cap].astype(F32)
        for ref, size in ((lines_ref, 0), (relay_ref, q.spare), (near_ref, q.near_front))
    )
    flag_ref[...] = jnp.maximum(own_flag_ref[...], jnp.broadcast_to(cross3[3:4, 0:128], flag_ref.shape))
    cross2, cross3, near = cross2[0:2], cross3[4:6], near[0:2]
    tags = jnp.concatenate(
        [
            cross2[:, q.each :],
            cross2[:, : q.front],
            cross3[:, : q.front],
            near[:, : q.near_front],
            cross3[:, q.each :],
            cross2[:, q.front : q.each],
            cross3[:, q.front : q.each],
            near[:, q.near_front :],
        ],
        axis=1,
    )
    tags = jnp.concatenate([tags, jnp.zeros((LINES - 2, tags.shape[1]), F32)], axis=0)
    rows_ref[at : at + LINES, :] = jnp.zeros((LINES, rows_ref.shape[1]), BF)
    rows_ref[at : at + LINES, 0 : tags.shape[1]] = tags.astype(BF)


def segment_line(f, part):
    base = f * COLS + part * (COLS // 2)
    return (lax.broadcasted_iota(jnp.int32, (COLS // 2, 1), 0) + base).astype(F32)


def stack_into(out_ref, label, rows_ref, part):
    share = COLS // 2
    for f in range(FINE):
        chosen = one_hot(label == segment_line(f, part))
        out_ref[f * share : (f + 1) * share, :] = jnp.dot(
            chosen, rows_ref[...], preferred_element_type=F32
        ).astype(out_ref.dtype)


def stack_sent_kernel(q, *refs):
    *given, sent_ref, all_ref, labels_ref, tags_ref = refs
    labels, later, at = [], [], 0
    for ref, size in zip(given, (q.first, q.first, q.cap, q.cap)):
        labels.append(tag_of(ref[size : size + LINES, 0:size]))
        all_ref[at : at + size, :] = ref[0:size, :]
        at += size
    for ref in given[:2]:
        later.append(tag_of(ref[q.first : q.first + LINES, q.first : q.first + q.second]))
    label = jnp.concatenate(labels, axis=1)
    labels_ref[...] = jnp.broadcast_to(label, labels_ref.shape)
    tags_ref[...] = jnp.broadcast_to(jnp.concatenate(later, axis=1), tags_ref.shape)
    stack_into(sent_ref, label, all_ref, 1 - lax.axis_index("off"))


def stack_kept_kernel(all_ref, labels_ref, kept_ref):
    stack_into(kept_ref, labels_ref[0:1, :], all_ref, lax.axis_index("off"))


def join_kernel(*refs):
    *given, out_ref = refs
    at = 0
    for ref in given:
        out_ref[at : at + ref.shape[0], :] = ref[...]
        at += ref.shape[0]


def stack_second_kernel(q, tags_ref, kept_ref, own_ref, other_ref, out_ref, rows_ref):
    x = lax.axis_index("off")
    rows_ref[: q.second, :] = own_ref[...]
    rows_ref[q.second :, :] = other_ref[...]
    label = tags_ref[0:1, :]
    share = COLS // 2
    for f in range(FINE):
        span = slice(f * share, (f + 1) * share)
        more = jnp.dot(one_hot(label == segment_line(f, x)), rows_ref[...], preferred_element_type=F32)
        out_ref[span, :] = (kept_ref[span, :] + more).astype(BF)


def short_path(cap, records, mid_bin, live_count, fine_class, ops, index):
    q = Slots(cap)
    samples = records.shape[1]
    share, depth = COLS // 2, ops.shape[1] * ops.shape[-1]
    packed, lines, own, flag, held = pl.pallas_call(
        functools.partial(pack_spare_kernel, q),
        out_shape=[
            shape(q.spare, samples),
            shape(LINES, TILE),
            shape(q.cap + LINES, samples),
            shape(8, 128, F32),
            shape(*records.shape),
        ],
        in_specs=[smem()] + [pl.BlockSpec(memory_space=pltpu.HBM)] * 3,
        out_specs=[vmem()] * 5,
        scratch_shapes=[
            pltpu.VMEM(mid_bin.shape, jnp.int32),
            pltpu.VMEM(fine_class.shape, jnp.int32),
            pltpu.SemaphoreType.DMA((10,)),
        ],
        compiler_params=params(24),
        name="pack_spare",
    )(live_count, mid_bin, fine_class, records)
    spare, lines, own_other = swap(packed, "bin", 2), swap(lines, "bin", 2), swap(own, "sub", 1)
    cross2, cross3, near, back2, back3, near_back = call(
        functools.partial(pack_rest_kernel, q),
        [shape(q.front, samples)] * 2
        + [shape(q.near_front + LINES, samples)]
        + [shape(q.back, samples)] * 2
        + [shape(q.near_back, samples)],
        [live_count, mid_bin, fine_class, held],
        1,
        "pack_rest",
        flops=2 * (2 * q.each + q.cap) * records.size,
        after=[packed],
    )
    cross2, cross3, near = swap(cross2, "bin", 2), swap(cross3, "bin", 3), swap(near, "bin", 1)
    for axis in ("sub", "off", "grp"):
        mask = 1
        while mask < lax.axis_size(axis):
            flag = jnp.maximum(flag, swap(flag, axis, mask))
            mask *= 2
    (relay,) = call(
        functools.partial(relay_kernel, q), [shape(q.spare + LINES, samples)], [spare, lines, flag], 0, "relay"
    )
    relay = swap(relay, "bin", 1)
    back2, back3, near_back = gate([back2, back3, near_back], [cross3])
    rows, flag = call(
        functools.partial(gather_kernel, q),
        [shape(q.first + LINES, samples), shape(8, 128, F32)],
        [spare, lines, cross2, cross3, near, relay, flag],
        0,
        "gather",
        after=[back2, own_other],
    )
    flag = jnp.maximum(flag, swap(flag, "bin", 2))
    back2, back3, near_back = swap(back2, "bin", 2), swap(back3, "bin", 3), swap(near_back, "bin", 1)
    given = [rows, swap(rows, "sub", 1), own, own_other]
    slots = 2 * (q.first + q.cap)
    flops = FINE * COLS * slots * samples
    sent, every, labels, tags = call(
        functools.partial(stack_sent_kernel, q),
        [
            shape(FINE * share, samples),
            shape(slots, samples),
            shape(8, slots, F32),
            shape(8, 2 * q.second, F32),
        ],
        given,
        0,
        "stack_sent",
        flops=flops,
        after=[flag],
    )
    terms = call(
        send_kernel,
        [shape(share, depth // 2)] * 2,
        [index, ops, sent],
        1,
        "operate",
        flops=2 * share * ops.size,
    )
    came = [swap(piece, "off", 1) for piece in terms]
    (kept,) = call(
        stack_kept_kernel,
        [shape(FINE * share, samples, F32)],
        [every, labels],
        0,
        "stack_kept",
        flops=flops,
        after=[terms[0]],
    )
    (late,) = call(
        join_kernel,
        [shape(q.second, samples)],
        [back2, back3, near_back],
        0,
        "join",
        after=[kept, *came],
    )
    (stacked,) = call(
        functools.partial(stack_second_kernel, q),
        [shape(FINE * share, samples)],
        [tags, kept, late, swap(late, "sub", 1)],
        0,
        "stack_second",
        scratch=[pltpu.VMEM((2 * q.second, samples), BF)],
        flops=2 * FINE * COLS * q.second * samples,
    )
    (image,) = call(
        finish_kernel,
        [shape(share, depth, F32)],
        [index, ops, stacked, *came],
        1,
        "finish",
        flops=2 * share * ops.size,
    )
    given = (records, mid_bin, live_count, fine_class, ops, index)
    return lax.cond(flag[0, 0] > 0.0, lambda image, *a: static_path(cap, *a), lambda image, *a: image, image, *given)


def local(traces, mid_bin, live_count, fine_class, operator, block_index):
    records = traces[0]
    owners, offs = lax.axis_size("bin"), lax.axis_size("off")
    cap = 3 * records.shape[0] // (2 * owners)
    path = short_path if owners == 4 and offs == 2 else static_path
    return path(cap, records, mid_bin, live_count, fine_class, operator[0, :, 0], block_index[0, :, 0])


def solution(mesh):
    placed = (
        P(("grp", "off"), ("bin", "sub"), None),
        P(("grp", "off"), ("bin", "sub")),
        P(("grp", "off"), ("bin", "sub")),
        P(("grp", "off"), ("bin", "sub")),
        P(("grp", "off"), None, "bin", "sub", None, None, None),
        P(("grp", "off"), None, "bin", "sub", None),
    )
    return jax.shard_map(
        local,
        mesh=mesh,
        in_specs=placed,
        out_specs=P(("grp", "bin", "off"), "sub"),
        check_vma=False,
    )
```

```python
import functools

import jax
import jax.numpy as jnp
from jax import lax
from jax.experimental import pallas as pl
from jax.experimental.pallas import tpu as pltpu
from jax.sharding import PartitionSpec as P

FINE = 2
COLS = 512
LINES = 16
TILE = 256
BF = jnp.bfloat16
F32 = jnp.float32
MIB = 1 << 20


def params(mib):
    return pltpu.CompilerParams(vmem_limit_bytes=mib * MIB)


def vmem():
    return pl.BlockSpec(memory_space=pltpu.VMEM)


def smem():
    return pl.BlockSpec(memory_space=pltpu.SMEM)


def call(body, out_shape, operands, scalars, name, mib=24, scratch=(), flops=0, after=()):
    moved = sum(a.size * a.dtype.itemsize for a in (*operands, *out_shape))
    count, late = len(operands), len(after)

    def run(*refs):
        body(*refs[:count], *refs[count + late :])

    return pl.pallas_call(
        run,
        out_shape=list(out_shape),
        in_specs=[smem()] * scalars + [vmem()] * (count - scalars + late),
        out_specs=[vmem()] * len(out_shape),
        scratch_shapes=list(scratch),
        compiler_params=params(mib),
        cost_estimate=pl.CostEstimate(flops=flops, bytes_accessed=moved, transcendentals=0),
        name=name,
    )(*operands, *(corner(a) for a in after))


def corner(a):
    return a[:LINES, :128]


def gate(given, after):
    return pl.pallas_call(
        lambda *refs: None,
        out_shape=[jax.ShapeDtypeStruct(a.shape, a.dtype) for a in given],
        in_specs=[vmem()] * (len(given) + len(after)),
        out_specs=[vmem()] * len(given),
        input_output_aliases={i: i for i in range(len(given))},
        compiler_params=params(4),
        cost_estimate=pl.CostEstimate(flops=0, bytes_accessed=0, transcendentals=0),
        name="gate",
    )(*given, *(corner(a) for a in after))


def shape(rows, columns, kind=BF):
    return jax.ShapeDtypeStruct((rows, columns), kind)


def one_hot(mask):
    return jnp.where(mask, 1.0, 0.0).astype(BF)


def running_count(mask_rows):
    rows = mask_rows.shape[1]
    upper = lax.broadcasted_iota(jnp.int32, (rows, rows), 0) <= lax.broadcasted_iota(jnp.int32, (rows, rows), 1)
    return jnp.dot(one_hot(mask_rows), one_hot(upper), preferred_element_type=F32)


def choose(position, slots):
    place = lax.broadcasted_iota(jnp.int32, (slots, position.shape[1]), 0).astype(F32)
    return one_hot(position == place)


def tag_digits(live, owner, mid, fine, lines=LINES):
    tag = jnp.where(live, fine * COLS + mid - owner * COLS + 1, 0)
    line = lax.broadcasted_iota(jnp.int32, (lines, tag.shape[1]), 0)
    return jnp.where(line == 0, tag // 256, jnp.where(line == 1, tag % 256, 0)).astype(F32).astype(BF)


def across(digits, chosen):
    return lax.dot_general(digits, chosen, (((1,), (1,)), ((), ())), preferred_element_type=F32)


def tag_of(lines):
    lines = lines.astype(F32)
    return 256.0 * lines[0:1] + lines[1:2] - 1.0


def full_pack_kernel(owners, cap, live_ref, mid_ref, fine_ref, traces_ref, *outs):
    z = lax.axis_index("bin")
    rows, samples = traces_ref.shape
    live = lax.broadcasted_iota(jnp.int32, (1, rows), 1) < live_ref[0, 0]
    mid = mid_ref[...]
    owner = mid // COLS
    target = lax.broadcasted_iota(jnp.int32, (max(owners, 16), rows), 0) ^ z
    hits = jnp.where(live, owner, -1) == target
    slot = jnp.where(hits, running_count(hits) - 1.0, -1.0)
    digits = tag_digits(live, owner, mid, fine_ref[...])
    for d in range(owners):
        select = choose(slot[d : d + 1], cap)
        outs[d][0:cap, :] = jnp.dot(select, traces_ref[...], preferred_element_type=F32).astype(BF)
        outs[d][cap : cap + LINES, :] = jnp.zeros((LINES, samples), BF)
        outs[d][cap : cap + LINES, 0:cap] = across(digits, select).astype(BF)


def full_stack_kernel(cap, *refs):
    *given, stacked_ref, rows_ref = refs
    label = jnp.concatenate([tag_of(ref[cap : cap + LINES, 0:cap]) for ref in given], axis=1)
    for i, ref in enumerate(given):
        rows_ref[i * cap : (i + 1) * cap, :] = ref[0:cap, :]

    def tile(t, carry):
        base = pl.multiple_of(t * TILE, TILE)
        line = (lax.broadcasted_iota(jnp.int32, (TILE, 1), 0) + base).astype(F32)
        stacked_ref[pl.ds(base, TILE), :] = jnp.dot(
            one_hot(label == line), rows_ref[...], preferred_element_type=F32
        ).astype(BF)
        return carry

    lax.fori_loop(0, FINE * COLS // TILE, tile, 0)


def image_terms(d, index_ref, ops_ref, stacked_ref):
    fine, _, taps = index_ref.shape
    width = ops_ref.shape[-1]
    columns = stacked_ref.shape[0] // fine
    picked, weights = [], []
    for f in range(fine):
        for k in range(taps):
            at = pl.multiple_of(index_ref[f, d, k] * width, width)
            picked.append(stacked_ref[f * columns : (f + 1) * columns, pl.ds(at, width)])
            weights.append(ops_ref[f, d, k])
    return lax.dot_general(
        jnp.concatenate(picked, axis=1),
        jnp.concatenate(weights, axis=1),
        (((1,), (1,)), ((), ())),
        preferred_element_type=F32,
    )


def operate_kernel(index_ref, ops_ref, stacked_ref, out_ref):
    width = ops_ref.shape[-1]
    for d in range(index_ref.shape[1]):
        terms = image_terms(d, index_ref, ops_ref, stacked_ref)
        out_ref[0 : terms.shape[0], d * width : (d + 1) * width] = terms.astype(out_ref.dtype)


def operate(index, ops, stacked, kind):
    columns, depth = stacked.shape[0] // FINE, ops.shape[1] * ops.shape[-1]
    (out,) = call(
        operate_kernel,
        [shape(columns, depth, kind)],
        [index, ops, stacked],
        1,
        "operate",
        flops=2 * columns * ops.size,
    )
    return out


def send_kernel(index_ref, ops_ref, stacked_ref, *outs):
    width = ops_ref.shape[-1]
    each = outs[0].shape[1]
    for d in range(index_ref.shape[1]):
        piece, at = outs[d * width // each], d * width % each
        piece[:, at : at + width] = image_terms(d, index_ref, ops_ref, stacked_ref).astype(BF)


def finish_kernel(index_ref, ops_ref, stacked_ref, *refs):
    *came, out_ref = refs
    width = ops_ref.shape[-1]
    each = came[0].shape[1]
    for d in range(index_ref.shape[1]):
        piece, at = came[d * width // each], d * width % each
        more = piece[:, at : at + width].astype(F32)
        out_ref[:, d * width : (d + 1) * width] = image_terms(d, index_ref, ops_ref, stacked_ref) + more


def swap(x, axis, mask):
    return lax.ppermute(x, axis, [(i, i ^ mask) for i in range(lax.axis_size(axis))])


def static_path(cap, records, mid_bin, live_count, fine_class, ops, index):
    owners, subs, offs = (lax.axis_size(a) for a in ("bin", "sub", "off"))
    samples = records.shape[1]
    packed = call(
        functools.partial(full_pack_kernel, owners, cap),
        [shape(cap + LINES, samples)] * owners,
        [live_count, mid_bin, fine_class, records],
        1,
        "full_pack",
    )
    arrived = [packed[0]] + [swap(packed[d], "bin", d) for d in range(1, owners)]
    arrived += [swap(a, "sub", e) for e in range(1, subs) for a in arrived]
    (stacked,) = call(
        functools.partial(full_stack_kernel, cap),
        [shape(FINE * COLS, samples)],
        arrived,
        0,
        "full_stack",
        mib=32,
        scratch=[pltpu.VMEM((cap * len(arrived), samples), BF)],
    )
    terms = operate(index, ops, stacked, F32)
    share = COLS // offs
    x = lax.axis_index("off")
    total = lax.dynamic_slice_in_dim(terms, x * share, share, axis=0)
    for k in range(1, offs):
        total = total + swap(lax.dynamic_slice_in_dim(terms, (x ^ k) * share, share, axis=0), "off", k)
    return total


class Slots:
    def __init__(self, cap):
        self.cap = cap
        self.each = 2 * cap // 3
        self.spare = cap - self.each
        self.front = 5 * cap // 12
        self.back = self.each - self.front
        self.near_front = 2 * cap // 3
        self.near_back = cap - self.near_front
        self.first = 2 * self.spare + 2 * self.front + self.near_front
        self.second = 2 * self.back + self.near_back


def positions(q, live_ref, mid_ref):
    rows = mid_ref.shape[1]
    z, x = lax.axis_index("bin"), lax.axis_index("off")
    live = lax.broadcasted_iota(jnp.int32, (1, rows), 1) < live_ref[0, 0]
    mid = mid_ref[...]
    owner = mid // COLS
    share = COLS // 2
    kept = jnp.where((mid - owner * COLS) // share == x, 1, 0)
    kind = jnp.where(live, (owner ^ z) * 2 + kept, -1)
    hits = lax.broadcasted_iota(jnp.int32, (16, rows), 0) == kind
    rank = running_count(hits)
    seat = jnp.where(hits, rank - 1.0, -1.0)
    place, late, spare = [], [], -1.0
    base = jnp.zeros((1, 1), F32)
    for d in range(4):
        first, second = seat[2 * d : 2 * d + 1], seat[2 * d + 1 : 2 * d + 2]
        if d < 2:
            place.append(jnp.where(first >= 0, first, jnp.where(second >= 0, q.cap - 1.0 - second, -1.0)))
            continue
        ahead = rank[2 * d : 2 * d + 1, rows - 1 : rows]
        behind = rank[2 * d + 1 : 2 * d + 2, rows - 1 : rows]
        room = q.each - jnp.minimum(ahead, float(q.front))
        late_first, late_second = first >= q.front, second >= room
        place.append(
            jnp.where(
                late_first | late_second, -1.0, jnp.where(first >= 0, first, jnp.where(second >= 0, q.each - 1.0 - second, -1.0))
            )
        )
        late.append(late_first | late_second)
        over = jnp.maximum(ahead - q.front, 0.0)
        spare = jnp.where(
            late_first, base + first - q.front, jnp.where(late_second, base + over + second - room, spare)
        )
        base = base + over + jnp.maximum(behind - room, 0.0)
    excess = jnp.maximum(base - q.spare, rank[2:3, rows - 1 : rows] - q.near_front)
    return live, mid, owner, place, spare, late, excess


def lay(ref, rows, tags):
    size = rows.shape[0]
    ref[0:size, :] = rows
    ref[size : size + LINES, :] = jnp.zeros((LINES, ref.shape[1]), BF)
    ref[size : size + LINES, 0 : tags.shape[1]] = tags.astype(BF)


def pack_spare_kernel(
    q, live_ref, mid_hbm, fine_hbm, traces_ref, spare_ref, lines_ref, own_ref, flag_ref, held_ref, mid_ref, fine_ref, sems
):
    copies = [
        pltpu.make_async_copy(mid_hbm, mid_ref, sems.at[0]),
        pltpu.make_async_copy(fine_hbm, fine_ref, sems.at[1]),
    ]
    count = sems.shape[0] - 2
    step = held_ref.shape[0] // count
    for i in range(count):
        span = pl.ds(i * step, step)
        copies.append(pltpu.make_async_copy(traces_ref.at[span], held_ref.at[span], sems.at[i + 2]))
    for copy in copies:
        copy.start()
    for copy in copies[:2]:
        copy.wait()
    live, mid, owner, place, spare, late, excess = positions(q, live_ref, mid_ref)
    digits = tag_digits(live, owner, mid, fine_ref[...])
    extra = [choose(jnp.where(late[i], spare, -1.0), q.spare) for i in range(2)]
    tags = [across(digits, jnp.concatenate([choose(place[d], q.each), extra[d - 2]], axis=0)) for d in (2, 3)]
    crossing = jnp.concatenate([tags[0][0:4], tags[1][0:4], jnp.zeros((LINES - 8, q.cap), F32)], axis=0)
    own = choose(place[0], q.cap)
    chosen = jnp.concatenate([extra[0] + extra[1], own], axis=0)
    lines_ref[...] = jnp.zeros(lines_ref.shape, BF)
    lines_ref[:, 0 : q.cap] = crossing.astype(BF)
    for copy in copies[2:]:
        copy.wait()
    rows = jnp.dot(chosen, held_ref[...], preferred_element_type=F32).astype(BF)
    spare_ref[...] = rows[: q.spare]
    lay(own_ref, rows[q.spare :], across(digits, own))
    flag_ref[...] = jnp.broadcast_to(jnp.where(excess > 0.0, 1.0, 0.0), flag_ref.shape)


def pack_rest_kernel(
    q, live_ref, mid_ref, fine_ref, traces_ref, cross2_ref, cross3_ref, near_ref, back2_ref, back3_ref, near_back_ref
):
    live, mid, owner, place, _, _, _ = positions(q, live_ref, mid_ref)
    digits = tag_digits(live, owner, mid, fine_ref[...])
    near = choose(place[1], q.cap)
    chosen = jnp.concatenate([choose(place[2], q.each), choose(place[3], q.each), near], axis=0)
    rows = jnp.dot(chosen, traces_ref[...], preferred_element_type=F32).astype(BF)
    cross2_ref[...] = rows[: q.front]
    back2_ref[...] = rows[q.front : q.each]
    cross3_ref[...] = rows[q.each : q.each + q.front]
    back3_ref[...] = rows[q.each + q.front : 2 * q.each]
    at = 2 * q.each + q.near_front
    lay(near_ref, rows[2 * q.each : at], across(digits, near))
    near_back_ref[...] = rows[at:]


def relay_kernel(q, spare_ref, lines_ref, flag_ref, out_ref):
    out_ref[0 : q.spare, :] = spare_ref[...]
    row = lax.broadcasted_iota(jnp.int32, lines_ref.shape, 0)
    out_ref[q.spare : q.spare + LINES, :] = jnp.zeros((LINES, out_ref.shape[1]), BF)
    out_ref[q.spare : q.spare + LINES, 0 : lines_ref.shape[1]] = jnp.where(
        row == 3, flag_ref[0:1, 0:1].astype(BF), lines_ref[...]
    )


def gather_kernel(
    q, spare_ref, lines_ref, cross2_ref, cross3_ref, near_ref, relay_ref, own_flag_ref, rows_ref, flag_ref
):
    at = 0
    for ref, size in (
        (spare_ref, q.spare),
        (cross2_ref, q.front),
        (cross3_ref, q.front),
        (near_ref, q.near_front),
        (relay_ref, q.spare),
    ):
        rows_ref[at : at + size, :] = ref[0:size, :]
        at += size
    cross2, cross3, near = (
        ref[size : size + LINES, 0 : q.cap].astype(F32)
        for ref, size in ((lines_ref, 0), (relay_ref, q.spare), (near_ref, q.near_front))
    )
    flag_ref[...] = jnp.maximum(own_flag_ref[...], jnp.broadcast_to(cross3[3:4, 0:128], flag_ref.shape))
    cross2, cross3, near = cross2[0:2], cross3[4:6], near[0:2]
    tags = jnp.concatenate(
        [
            cross2[:, q.each :],
            cross2[:, : q.front],
            cross3[:, : q.front],
            near[:, : q.near_front],
            cross3[:, q.each :],
            cross2[:, q.front : q.each],
            cross3[:, q.front : q.each],
            near[:, q.near_front :],
        ],
        axis=1,
    )
    tags = jnp.concatenate([tags, jnp.zeros((LINES - 2, tags.shape[1]), F32)], axis=0)
    rows_ref[at : at + LINES, :] = jnp.zeros((LINES, rows_ref.shape[1]), BF)
    rows_ref[at : at + LINES, 0 : tags.shape[1]] = tags.astype(BF)


def segment_line(f, part):
    base = f * COLS + part * (COLS // 2)
    return (lax.broadcasted_iota(jnp.int32, (COLS // 2, 1), 0) + base).astype(F32)


def stack_into(out_ref, label, rows_ref, part):
    share = COLS // 2
    for f in range(FINE):
        chosen = one_hot(label == segment_line(f, part))
        out_ref[f * share : (f + 1) * share, :] = jnp.dot(
            chosen, rows_ref[...], preferred_element_type=F32
        ).astype(out_ref.dtype)


def stack_sent_kernel(q, *refs):
    *given, sent_ref, all_ref, labels_ref, tags_ref = refs
    labels, later, at = [], [], 0
    for ref, size in zip(given, (q.first, q.first, q.cap, q.cap)):
        labels.append(tag_of(ref[size : size + LINES, 0:size]))
        all_ref[at : at + size, :] = ref[0:size, :]
        at += size
    for ref in given[:2]:
        later.append(tag_of(ref[q.first : q.first + LINES, q.first : q.first + q.second]))
    label = jnp.concatenate(labels, axis=1)
    labels_ref[...] = jnp.broadcast_to(label, labels_ref.shape)
    tags_ref[...] = jnp.broadcast_to(jnp.concatenate(later, axis=1), tags_ref.shape)
    stack_into(sent_ref, label, all_ref, 1 - lax.axis_index("off"))


def stack_kept_kernel(all_ref, labels_ref, kept_ref):
    stack_into(kept_ref, labels_ref[0:1, :], all_ref, lax.axis_index("off"))


def join_kernel(*refs):
    *given, out_ref = refs
    at = 0
    for ref in given:
        out_ref[at : at + ref.shape[0], :] = ref[...]
        at += ref.shape[0]


def stack_second_kernel(q, tags_ref, kept_ref, own_ref, other_ref, out_ref, rows_ref):
    x = lax.axis_index("off")
    rows_ref[: q.second, :] = own_ref[...]
    rows_ref[q.second :, :] = other_ref[...]
    label = tags_ref[0:1, :]
    share = COLS // 2
    for f in range(FINE):
        span = slice(f * share, (f + 1) * share)
        more = jnp.dot(one_hot(label == segment_line(f, x)), rows_ref[...], preferred_element_type=F32)
        out_ref[span, :] = (kept_ref[span, :] + more).astype(BF)


def short_path(cap, records, mid_bin, live_count, fine_class, ops, index):
    q = Slots(cap)
    samples = records.shape[1]
    share, depth = COLS // 2, ops.shape[1] * ops.shape[-1]
    packed, lines, own, flag, held = pl.pallas_call(
        functools.partial(pack_spare_kernel, q),
        out_shape=[
            shape(q.spare, samples),
            shape(LINES, TILE),
            shape(q.cap + LINES, samples),
            shape(8, 128, F32),
            shape(*records.shape),
        ],
        in_specs=[smem()] + [pl.BlockSpec(memory_space=pltpu.HBM)] * 3,
        out_specs=[vmem()] * 5,
        scratch_shapes=[
            pltpu.VMEM(mid_bin.shape, jnp.int32),
            pltpu.VMEM(fine_class.shape, jnp.int32),
            pltpu.SemaphoreType.DMA((10,)),
        ],
        compiler_params=params(24),
        name="pack_spare",
    )(live_count, mid_bin, fine_class, records)
    spare, lines, own_other = swap(packed, "bin", 2), swap(lines, "bin", 2), swap(own, "sub", 1)
    cross2, cross3, near, back2, back3, near_back = call(
        functools.partial(pack_rest_kernel, q),
        [shape(q.front, samples)] * 2
        + [shape(q.near_front + LINES, samples)]
        + [shape(q.back, samples)] * 2
        + [shape(q.near_back, samples)],
        [live_count, mid_bin, fine_class, held],
        1,
        "pack_rest",
        flops=2 * (2 * q.each + q.cap) * records.size,
        after=[packed],
    )
    cross2, cross3, near = swap(cross2, "bin", 2), swap(cross3, "bin", 3), swap(near, "bin", 1)
    for axis in ("sub", "off", "grp"):
        mask = 1
        while mask < lax.axis_size(axis):
            flag = jnp.maximum(flag, swap(flag, axis, mask))
            mask *= 2
    (relay,) = call(
        functools.partial(relay_kernel, q), [shape(q.spare + LINES, samples)], [spare, lines, flag], 0, "relay", after=[own_other]
    )
    relay = swap(relay, "bin", 1)
    back2, back3, near_back = gate([back2, back3, near_back], [cross3])
    rows, flag = call(
        functools.partial(gather_kernel, q),
        [shape(q.first + LINES, samples), shape(8, 128, F32)],
        [spare, lines, cross2, cross3, near, relay, flag],
        0,
        "gather",
        after=[back2],
    )
    flag = jnp.maximum(flag, swap(flag, "bin", 2))
    back2, back3, near_back = swap(back2, "bin", 2), swap(back3, "bin", 3), swap(near_back, "bin", 1)
    given = [rows, swap(rows, "sub", 1), own, own_other]
    slots = 2 * (q.first + q.cap)
    flops = FINE * COLS * slots * samples
    sent, every, labels, tags = call(
        functools.partial(stack_sent_kernel, q),
        [
            shape(FINE * share, samples),
            shape(slots, samples),
            shape(8, slots, F32),
            shape(8, 2 * q.second, F32),
        ],
        given,
        0,
        "stack_sent",
        flops=flops,
        after=[flag],
    )
    terms = call(
        send_kernel,
        [shape(share, depth // 2)] * 2,
        [index, ops, sent],
        1,
        "operate",
        flops=2 * share * ops.size,
    )
    came = [swap(piece, "off", 1) for piece in terms]
    (kept,) = call(
        stack_kept_kernel,
        [shape(FINE * share, samples, F32)],
        [every, labels],
        0,
        "stack_kept",
        flops=flops,
        after=[terms[0]],
    )
    (late,) = call(
        join_kernel,
        [shape(q.second, samples)],
        [back2, back3, near_back],
        0,
        "join",
        after=[kept, *came],
    )
    (stacked,) = call(
        functools.partial(stack_second_kernel, q),
        [shape(FINE * share, samples)],
        [tags, kept, late, swap(late, "sub", 1)],
        0,
        "stack_second",
        scratch=[pltpu.VMEM((2 * q.second, samples), BF)],
        flops=2 * FINE * COLS * q.second * samples,
    )
    (image,) = call(
        finish_kernel,
        [shape(share, depth, F32)],
        [index, ops, stacked, *came],
        1,
        "finish",
        flops=2 * share * ops.size,
    )
    given = (records, mid_bin, live_count, fine_class, ops, index)
    return lax.cond(flag[0, 0] > 0.0, lambda image, *a: static_path(cap, *a), lambda image, *a: image, image, *given)


def local(traces, mid_bin, live_count, fine_class, operator, block_index):
    records = traces[0]
    owners, offs = lax.axis_size("bin"), lax.axis_size("off")
    cap = 3 * records.shape[0] // (2 * owners)
    path = short_path if owners == 4 and offs == 2 else static_path
    return path(cap, records, mid_bin, live_count, fine_class, operator[0, :, 0], block_index[0, :, 0])


def solution(mesh):
    placed = (
        P(("grp", "off"), ("bin", "sub"), None),
        P(("grp", "off"), ("bin", "sub")),
        P(("grp", "off"), ("bin", "sub")),
        P(("grp", "off"), ("bin", "sub")),
        P(("grp", "off"), None, "bin", "sub", None, None, None),
        P(("grp", "off"), None, "bin", "sub", None),
    )
    return jax.shard_map(
        local,
        mesh=mesh,
        in_specs=placed,
        out_specs=P(("grp", "bin", "off"), "sub"),
        check_vma=False,
    )
```
